256 devices in a mesh: dp: 32 (over z_lo, y, core), expert: 4 (over x), rollout: 2 (over z_hi).
Axes of the slice: x: 4, y: 4, z: 8 (z_hi: 2, z_lo: 4; z = z_hi * 4 + z_lo), core: 2. Of those that a mesh axis runs over, the one named last changes fastest.
Arguments:
- hidden: bfloat16 [16, 20480, 1536], P('expert', ('dp', 'rollout')), may hold values from -16 to 16
- slot_token: int32 [16, 20480], P('expert', ('dp', 'rollout')), may hold values from 0 to 511, as said below
- gate: float32 [16, 20480], P('expert', ('dp', 'rollout')), may hold values from 0.05 to 1
- counts: int32 [16, 64], P('expert', ('dp', 'rollout')), may hold values from 106 to 320, as said below
- cotangent: bfloat16 [32768, 4096], P(('dp', 'rollout')), may hold values from -0.02734375 to 0.02734375
- halfwidth_replica: bfloat16 [5632, 1024], P(None, 'expert'), may hold values from -0.59765625 to 0.59765625
- precise_matrices: float32 [5632, 1024], P(('dp', 'rollout'), 'expert'), may hold values from -0.6 to 0.6
- running_mean: float32 [5632, 1024], P(('dp', 'rollout'), 'expert'), may hold values from -0.6 to 0.6
- running_variance: float32 [5632, 1024], P(('dp', 'rollout'), 'expert'), may hold values from 0.01 to 1
- base: bfloat16 [16, 1536, 4096], P('expert', 'rollout', 'dp'), may hold values from -0.95703125 to 0.95703125
Outputs:
- merged: bfloat16 [16, 1536, 4096], P('expert', None, 'dp')
- revised_precise: float32 [5632, 1024], P(('dp', 'rollout'), 'expert')
- new_first: float32 [5632, 1024], P(('dp', 'rollout'), 'expert')
- new_second: float32 [5632, 1024], P(('dp', 'rollout'), 'expert')
The draws below stay inside these ranges and needn't reach their ends.
Inputs may be any that keep to these rules, and one draw needn't show every extreme that they name: Slot s of expert e is live when (s mod 320) < counts[e, s div 320]; in every column of counts some expert has all 320 slots live. `slot_token`: indexes the cotangent rows of the same device group; within each aligned block of 320 slots of one expert on one device all entries are distinct.
All inputs are finite; a program needn't handle non-finite values.
Results may differ from the reference program's by a relative error of at most 0.005.
Values may be sent and summed in bfloat16 or wider, within the bound.
A program may use at most 128 MiB of HBM per device.

```python
import math
import jax
import jax.numpy as jnp
from jax import lax

EMBED_SIZE = 4096
INNER_NEURONS = 1536
LOWRANK_INNER = 64
CAP = 320
TOK_DEV = 512
STEP = 100
SPECIALIST_TALLY = 16
GROUPS = 64
SLOTS = 20480
TOKENS = 32768


def draw_counts(key, part):
    key = jax.random.fold_in(key, 7)
    spread_key, full_key = jax.random.split(key)
    spread = jax.random.randint(spread_key, (SPECIALIST_TALLY, GROUPS), CAP // 3, CAP + 1)
    fullest = jax.random.randint(full_key, (1, GROUPS), 0, SPECIALIST_TALLY)
    expert_rows = lax.broadcasted_iota(jnp.int32, (SPECIALIST_TALLY, GROUPS), 0)
    return jnp.where(expert_rows == fullest, CAP, spread).astype(jnp.int32)


def draw_slot_token(key, part):
    key = jax.random.fold_in(key, 11)
    block_keys = jax.random.split(key, SPECIALIST_TALLY * GROUPS)

    def pick_rows(block_key):
        order = jax.random.permutation(block_key, jnp.arange(TOK_DEV, dtype=jnp.int32))
        return order[:CAP]
    chosen = jax.vmap(pick_rows)(block_keys).reshape(SPECIALIST_TALLY, GROUPS, CAP)
    present = jnp.any(chosen == TOK_DEV - 1, axis=2)
    expert_rows = lax.broadcasted_iota(jnp.int32, (SPECIALIST_TALLY, GROUPS), 0)
    first_slot = jnp.where(jnp.logical_and(expert_rows == 0, jnp.logical_not(present)), TOK_DEV - 1, chosen[:, :, 0])
    chosen = jnp.concatenate([first_slot[:, :, None], chosen[:, :, 1:]], axis=2)
    return chosen.reshape(SPECIALIST_TALLY, GROUPS * CAP).astype(jnp.int32)


def spiked(drawn, key, source, target, shards_of, factor):
    owner, partner = [(jnp.arange(drawn.shape[position]) // (drawn.shape[position] // shards_of)).reshape([-1 if axis == position else 1 for axis in range(drawn.ndim)]) for position in (source, target)]
    chosen = jax.random.permutation(key, shards_of)[partner]
    strong = (owner == chosen) | (owner == (partner + shards_of // 2) % shards_of)
    return jnp.where(strong, factor * drawn, drawn)


def levels(stream_key, extent, cuts, smallest, high):
    gain, own = 1.0, jax.random.fold_in(stream_key, 6)
    for dim, shards_of in cuts:
        steps = jnp.exp(jax.random.uniform(jax.random.fold_in(own, dim), (shards_of,), jnp.float32, smallest / len(cuts), high / len(cuts)))
        gain = gain * jnp.repeat(steps, extent[dim] // shards_of).reshape([-1 if axis == dim else 1 for axis in range(len(extent))])
    return gain


def scatter_about(own_key, extent, width, most, pieces=(), kind=jnp.bfloat16):
    array = jax.random.normal(own_key, extent, jnp.float32) * width
    if len(pieces) > 0:
        array = levels(own_key, extent, pieces, -0.22, 0.18) * array
    return jnp.clip(array, min=-most, max=most).astype(kind)


def heavy_noise(rng, dims, deviation, most, shards, heavy, kind=jnp.bfloat16):
    drawn = deviation * jax.random.normal(rng, dims, jnp.float32)
    if shards:
        drawn = drawn * levels(rng, dims, shards, -0.22, 0.18)
    return jnp.clip(spiked(drawn, jax.random.fold_in(rng, 3), *heavy), -most, most).astype(kind)


def setup_inputs(seed: int = 0) -> dict:
    keys = jax.random.split(jax.random.key(seed), 11)
    hidden = heavy_noise(keys[0], (SPECIALIST_TALLY, SLOTS, INNER_NEURONS), 1.0, 16.0, ((0, 4), (1, 64)), (1, 2, 64, 4.0))
    slot_token = draw_slot_token(jax.random.fold_in(keys[10], 71), 0)
    gate = jnp.clip(jnp.exp(math.log(1.0) - 2.9957323 * jax.random.uniform(keys[2], (SPECIALIST_TALLY, SLOTS), jnp.float32) ** levels(keys[2], (SPECIALIST_TALLY, SLOTS), ((0, 4), (1, 64)), -0.2, 0.2)), 0.05, 1.0)
    counts = draw_counts(jax.random.fold_in(keys[10], 71), 0)
    cotangent = heavy_noise(keys[4], (TOKENS, EMBED_SIZE), (14.0 / (SLOTS * EMBED_SIZE) ** 0.5), 0.02734375, ((0, 64),), (0, 1, 64, 4.0))
    halfwidth_replica = scatter_about(keys[5], (INNER_NEURONS + EMBED_SIZE, SPECIALIST_TALLY * LOWRANK_INNER), 0.1, 0.59765625, ((1, 4),))
    precise_matrices = scatter_about(keys[6], (INNER_NEURONS + EMBED_SIZE, SPECIALIST_TALLY * LOWRANK_INNER), 0.1, 0.6, ((0, 64), (1, 4)), jnp.float32)
    running_mean = scatter_about(keys[7], (INNER_NEURONS + EMBED_SIZE, SPECIALIST_TALLY * LOWRANK_INNER), 0.1, 0.6, ((0, 64), (1, 4)), jnp.float32)
    running_variance = jnp.clip(jnp.exp(math.log(1.0) - 4.6051702 * jax.random.uniform(keys[8], (INNER_NEURONS + EMBED_SIZE, SPECIALIST_TALLY * LOWRANK_INNER), jnp.float32) ** levels(keys[8], (INNER_NEURONS + EMBED_SIZE, SPECIALIST_TALLY * LOWRANK_INNER), ((0, 64), (1, 4)), -0.2, 0.2)), 0.01, 1.0)
    base = scatter_about(keys[9], (SPECIALIST_TALLY, INNER_NEURONS, EMBED_SIZE), 0.16, 0.95703125, ((0, 4), (1, 2), (2, 32)))
    return dict(hidden=hidden, slot_token=slot_token, gate=gate, counts=counts, cotangent=cotangent, halfwidth_replica=halfwidth_replica, precise_matrices=precise_matrices, running_mean=running_mean, running_variance=running_variance, base=base)


delta_multiplier = 2.0
beta_first = 0.9
beta_second = 0.95
learn_rate = 0.04
decay_rate = 0.01
adam_eps = 1e-08

def adamw_update(derivative_total, precise_matrices, running_mean, running_variance):
    new_first = beta_first * running_mean + (1.0 - beta_first) * derivative_total
    new_second = beta_second * running_variance + (1.0 - beta_second) * derivative_total * derivative_total
    first_hat = new_first / (1.0 - beta_first ** STEP)
    second_hat = new_second / (1.0 - beta_second ** STEP)
    revised_precise = precise_matrices - learn_rate * (first_hat / (jnp.sqrt(second_hat) + adam_eps) + decay_rate * precise_matrices)
    return (revised_precise, new_first, new_second)

def expert_grad(inputs, cotangent):
    hidden_e, token_e, gate_e, count_e, factor_e = inputs
    first_factor = factor_e[:INNER_NEURONS]
    second_factor = factor_e[INNER_NEURONS:]

    def accumulate(totals, block_inputs):
        block_index, hidden_rows, token_rows, gate_block, live_count = block_inputs
        live_slots = jnp.arange(CAP, dtype=jnp.int32) < live_count
        masked = jnp.where(live_slots[:, None], hidden_rows, jnp.zeros((), hidden_rows.dtype))
        own_rows = lax.dynamic_slice_in_dim(cotangent, (block_index * TOK_DEV).astype(jnp.int32), TOK_DEV, 0)
        routed = (jnp.take(own_rows, token_rows, axis=0).astype(jnp.float32) * gate_block[:, None]).astype(jnp.bfloat16)
        down_proj = jnp.dot(masked, first_factor, preferred_element_type=jnp.float32).astype(jnp.bfloat16)
        back_proj = jnp.dot(routed, second_factor, preferred_element_type=jnp.float32).astype(jnp.bfloat16)
        first_total = totals[0] + jnp.dot(masked.T, back_proj, preferred_element_type=jnp.float32)
        second_total = totals[1] + jnp.dot(routed.T, down_proj, preferred_element_type=jnp.float32)
        return ((first_total, second_total), None)
    initial_tallies = (jnp.zeros((INNER_NEURONS, LOWRANK_INNER), jnp.float32), jnp.zeros((EMBED_SIZE, LOWRANK_INNER), jnp.float32))
    block_ids = jnp.arange(GROUPS, dtype=jnp.int32)
    totals, unused = lax.scan(accumulate, initial_tallies, (block_ids, hidden_e, token_e, gate_e, count_e))
    return jnp.concatenate([totals[0], totals[1]], axis=0)

def combine_tile(inputs):
    expert_base_weight, fresh_e = inputs
    rank_product = jnp.dot(fresh_e[:INNER_NEURONS], fresh_e[INNER_NEURONS:].T, preferred_element_type=jnp.float32)
    return (expert_base_weight.astype(jnp.float32) + delta_multiplier * rank_product).astype(jnp.bfloat16)

def reference(hidden, slot_token, gate, counts, cotangent, halfwidth_replica, precise_matrices, running_mean, running_variance, base):
    hidden_blocks = hidden.reshape(SPECIALIST_TALLY, GROUPS, CAP, INNER_NEURONS)
    token_blocks = slot_token.reshape(SPECIALIST_TALLY, GROUPS, CAP)
    gate_blocks = gate.reshape(SPECIALIST_TALLY, GROUPS, CAP)
    matrix_panels = halfwidth_replica.reshape(INNER_NEURONS + EMBED_SIZE, SPECIALIST_TALLY, LOWRANK_INNER).transpose(1, 0, 2)

    def one_expert(inputs):
        return expert_grad(inputs, cotangent)
    matrix_derivatives = lax.map(one_expert, (hidden_blocks, token_blocks, gate_blocks, counts, matrix_panels))
    derivative_total = delta_multiplier * matrix_derivatives.transpose(1, 0, 2).reshape(INNER_NEURONS + EMBED_SIZE, SPECIALIST_TALLY * LOWRANK_INNER)
    revised_precise, new_first, new_second = adamw_update(derivative_total, precise_matrices, running_mean, running_variance)
    renewed_matrices = revised_precise.astype(jnp.bfloat16).reshape(INNER_NEURONS + EMBED_SIZE, SPECIALIST_TALLY, LOWRANK_INNER).transpose(1, 0, 2)
    merged = lax.map(combine_tile, (base, renewed_matrices))
    return (merged, revised_precise, new_first, new_second)
```

```python
import functools

import jax
import jax.numpy as jnp
from jax import lax
from jax.experimental import pallas as pl
from jax.experimental.pallas import tpu as pltpu
from jax.sharding import PartitionSpec as P

STEP = 100

delta_multiplier = 2.0
beta_first = 0.9
beta_second = 0.95
learn_rate = 0.04
decay_rate = 0.01
adam_eps = 1e-08

MESH = pl.DeviceIdType.MESH
BF16 = jnp.bfloat16
F32 = jnp.float32

EXPERTS = 4
CAP = 320
SLOTS = EXPERTS * CAP
INNER = 1536
WIDE = 4096
TOK = 512
COLS = 256
ROWS = INNER + WIDE
SHARD = 88
PAIR = 2 * SHARD
TILE = 512
SPAN = 128
A_BLOCKS = 18


def adamw_update(derivative_total, precise_matrices, running_mean, running_variance):
    new_first = beta_first * running_mean + (1.0 - beta_first) * derivative_total
    new_second = (
        beta_second * running_variance + (1.0 - beta_second) * derivative_total * derivative_total
    )
    first_hat = new_first / (1.0 - beta_first**STEP)
    second_hat = new_second / (1.0 - beta_second**STEP)
    revised_precise = precise_matrices - learn_rate * (
        first_hat / (jnp.sqrt(second_hat) + adam_eps) + decay_rate * precise_matrices
    )
    return (revised_precise, new_first, new_second)


def fold(block):
    return jnp.concatenate([block[:, :128], block[:, 128:]], axis=0)


def unfold(block):
    return jnp.concatenate([block[:SHARD], block[SHARD:]], axis=1)


def dot(lhs, rhs):
    return jnp.dot(lhs, rhs, preferred_element_type=F32)


def dot_t(lhs, rhs):
    return lax.dot_general(lhs, rhs, (((0,), (0,)), ((), ())), preferred_element_type=F32)


def split(value):
    high = value.astype(BF16)
    return high, (value - high.astype(F32)).astype(BF16)


def exchange_kernel(
    hidden,
    slot_token,
    gate,
    counts,
    cotangent,
    factors,
    precise,
    mean,
    variance,
    base,
    base_other,
    fresh_main,
    fresh_extra,
    fresh_second,
    grad_out,
    hid,
    cot,
    fac,
    tok_v,
    gate_v,
    counts_v,
    opt_v,
    select,
    slots_v,
    grad,
    from_core,
    y_send,
    y_recv,
    z_keep,
    z_send,
    z_recv,
    fresh,
    load_sem,
    local_sem,
    base_sem,
    core_send_sem,
    core_recv_sem,
    y_send_sem,
    y_recv_sem,
    z_send_sem,
    z_recv_sem,
    az_send_sem,
    az_recv_sem,
    ay_send_sem,
    ay_recv_sem,
    ac_send_sem,
    ac_recv_sem,
    b_send_sem,
    b_recv_sem,
):
    dp = lax.axis_index("dp")
    half = lax.axis_index("rollout")
    core = lax.rem(dp, 2)
    row = lax.rem(lax.div(dp, 2), 4)
    low = lax.div(dp, 8)
    z = half * 4 + low
    mine = dp * 2 + half

    def device(c, y, zz):
        return {"dp": lax.rem(zz, 4) * 8 + y * 2 + c, "rollout": lax.div(zz, 4)}

    def at_y(step):
        return lax.rem(row + step, 4)

    def at_z(step):
        return lax.rem(z + step, 8)

    def remote(src, dst, send, recv, target):
        return pltpu.make_async_remote_copy(
            src_ref=src,
            dst_ref=dst,
            send_sem=send,
            recv_sem=recv,
            device_id=target,
            device_id_type=MESH,
        )

    loads = []

    def load(src, dst):
        copy = pltpu.make_async_copy(src, dst, load_sem.at[len(loads)])
        copy.start()
        loads.append(copy)
        return copy

    load_a = load(factors.at[pl.ds(0, INNER)], fac.at[pl.ds(0, INNER)])
    load_h = [
        load(hidden.at[e], hid.at[pl.ds(e * CAP, CAP)]) for e in range(EXPERTS)
    ]
    load_small = [load(slot_token, tok_v), load(gate, gate_v), load(counts, counts_v)]
    load_c = load(cotangent, cot)
    load_b = load(factors.at[pl.ds(INNER, WIDE)], fac.at[pl.ds(INNER, WIDE)])
    load_o = [
        load(precise, opt_v.at[0]),
        load(mean, opt_v.at[1]),
        load(variance, opt_v.at[2]),
    ]

    sends = []
    first_row = mine * SHARD - INNER
    first_user = lax.div(jnp.maximum(first_row, 0), SPAN)
    last_user = lax.div(jnp.maximum(first_row + SHARD - 1, 0), SPAN)
    has_second = first_row + SHARD > 0
    for q, user in enumerate((first_user, last_user)):
        wanted = has_second if q == 0 else jnp.logical_and(has_second, last_user != first_user)
        slot = mine - lax.div(INNER + SPAN * user, SHARD)
        for t in range(2):
            own = jnp.logical_and(user == dp, half == t)
            sends.append((user, t, slot, wanted, own))
    first_block = lax.div(INNER + SPAN * dp, SHARD)
    takes = []
    for j in range(3):
        block = first_block + j
        wanted = block * SHARD < INNER + SPAN * dp + SPAN
        takes.append((block, wanted, block == mine))

    barrier = pltpu.get_barrier_semaphore()

    def greet(target):
        pl.semaphore_signal(barrier, inc=1, device_id=target, device_id_type=MESH)

    greet(device(1 - core, row, z))
    for step in range(1, 4):
        greet(device(core, at_y(step), z))
    for step in range(1, 8):
        greet(device(core, row, at_z(step)))
    for user, t, slot, wanted, own in sends:

        @pl.when(jnp.logical_and(wanted, jnp.logical_not(own)))
        def _():
            greet({"dp": user, "rollout": t})

    for block, wanted, own in takes:

        @pl.when(jnp.logical_and(wanted, jnp.logical_not(own)))
        def _():
            greet({"dp": lax.div(block, 2), "rollout": lax.rem(block, 2)})

    greeted = 11
    for wanted, own in [s[3:] for s in sends] + [t[1:] for t in takes]:
        greeted = greeted + jnp.where(jnp.logical_and(wanted, jnp.logical_not(own)), 1, 0)
    pl.semaphore_wait(barrier, greeted)

    base_copy = remote(base, base_other, base_sem.at[0], base_sem.at[1], device(core, row, at_z(4)))
    base_copy.start()

    load_a.wait()
    lanes = lax.broadcasted_iota(jnp.int32, (CAP, COLS), 1)
    for e in range(EXPERTS):
        load_h[e].wait()
        down = dot(hid[e * CAP : (e + 1) * CAP], fac[:INNER])
        inside = jnp.logical_and(lanes >= e * 64, lanes < (e + 1) * 64)
        slots_v[e * CAP : (e + 1) * CAP] = jnp.where(inside, down, 0.0).astype(BF16)
    for copy in load_small:
        copy.wait()
    places = lax.broadcasted_iota(jnp.int32, (EXPERTS, CAP), 1)
    live_gate = jnp.where(places < counts_v[...], gate_v[...], 0.0)
    gate_high = live_gate.astype(BF16).astype(F32)
    gate_low = live_gate - gate_high
    tokens = lax.broadcasted_iota(jnp.int32, (TOK, CAP), 0)
    for e in range(EXPERTS):
        hit = tokens == tok_v[e : e + 1]
        for part, value in enumerate((gate_high, gate_low)):
            select[e, part] = jnp.where(hit, value[e : e + 1], 0.0).astype(BF16)
    by_token = jnp.zeros((TOK, COLS), F32)
    for e in range(EXPERTS):
        down = slots_v[e * CAP : (e + 1) * CAP]
        by_token = by_token + dot(select[e, 0], down) + dot(select[e, 1], down)
    token_high, token_low = split(by_token)

    load_c.wait()
    load_b.wait()
    back_high, back_low = split(dot(cot[...], fac[INNER:]))
    for e in range(EXPERTS):
        inside = jnp.logical_and(lanes >= e * 64, lanes < (e + 1) * 64)
        back = (
            dot_t(select[e, 0], back_high)
            + dot_t(select[e, 1], back_high)
            + dot_t(select[e, 0], back_low)
        )
        slots_v[e * CAP : (e + 1) * CAP] = jnp.where(inside, back, 0.0).astype(BF16)

    def core_copy(chunk):
        return remote(
            grad.at[pl.ds(pl.multiple_of(352 * chunk + PAIR * (1 - core), 8), PAIR)],
            from_core.at[chunk],
            core_send_sem.at[chunk],
            core_recv_sem.at[chunk],
            device(1 - core, row, z),
        )

    def own_rows(chunk):
        return grad[pl.ds(pl.multiple_of(352 * chunk + PAIR * core, 8), PAIR)]

    def y_copy(g, step):
        return remote(
            y_send.at[g, step - 1],
            y_recv.at[g, step - 1],
            y_send_sem.at[g, step - 1],
            y_recv_sem.at[g, step - 1],
            device(core, at_y(step), z),
        )

    def to_core(g):
        for chunk in range(4 * g, 4 * g + 4):
            core_copy(chunk).start()

    def to_y(g):
        for chunk in range(4 * g, 4 * g + 4):
            core_copy(chunk).wait_recv()
        for step in (2, 1, 3):
            chunk = 4 * g + at_y(step)
            y_send[g, step - 1] = (own_rows(chunk) + from_core[chunk]).astype(BF16)
            y_copy(g, step).start()

    for tile in range(3):
        grad[tile * TILE : (tile + 1) * TILE] = dot_t(
            hid[:, tile * TILE : (tile + 1) * TILE], slots_v[...]
        )
    to_core(0)

    def second_tile(tile):
        lhs = cot[:, tile * TILE : (tile + 1) * TILE]
        grad[INNER + tile * TILE : INNER + (tile + 1) * TILE] = dot_t(lhs, token_high) + dot_t(
            lhs, token_low
        )

    for tile in range(0, 3):
        second_tile(tile)
    to_core(1)
    to_y(0)
    for tile in range(3, 6):
        second_tile(tile)
    to_core(2)
    to_y(1)
    for tile in range(6, 8):
        second_tile(tile)
    to_core(3)
    to_y(2)
    to_y(3)

    def z_copy(step_index, block, target):
        return remote(
            z_send.at[block],
            z_recv.at[step_index],
            z_send_sem.at[step_index],
            z_recv_sem.at[step_index],
            device(core, row, target),
        )

    for g in range(4):
        for step in range(1, 4):
            y_copy(g, step).wait_recv()
        chunk = 4 * g + row
        total = own_rows(chunk) + from_core[chunk]
        for step in range(3):
            total = total + y_recv[g, step].astype(F32)
        for h in range(2):
            target = 4 * h + g
            block = fold(total[h * SHARD : (h + 1) * SHARD])
            z_keep[target] = block
            z_send[target] = block.astype(BF16)
            distance = lax.rem(target - z + 8, 8)

            @pl.when(distance != 0)
            def _():
                z_copy(distance - 1, target, target).start()

    derivative = z_keep[z]
    for step in range(1, 8):
        z_copy(step - 1, at_z(step), at_z(step)).wait_recv()
        derivative = derivative + z_recv[step - 1].astype(F32)
    derivative = delta_multiplier * unfold(derivative)
    for copy in load_o:
        copy.wait()
    revised, unused_first, unused_second = adamw_update(derivative, opt_v[0], opt_v[1], opt_v[2])
    fresh[...] = fold(revised).astype(BF16)
    z_keep[0] = fold(derivative)
    grad_copy = pltpu.make_async_copy(z_keep.at[0], grad_out, local_sem.at[5])
    grad_copy.start()

    for q, (user, t, slot, wanted, own) in enumerate(sends):
        copy = remote(
            fresh,
            fresh_second.at[slot],
            b_send_sem.at[q],
            b_recv_sem.at[slot],
            {"dp": user, "rollout": t},
        )

        @pl.when(jnp.logical_and(wanted, jnp.logical_not(own)))
        def _():
            copy.start()

        @pl.when(jnp.logical_and(wanted, own))
        def _():
            local = pltpu.make_async_copy(fresh, fresh_second.at[slot], local_sem.at[0])
            local.start()
            local.wait()

    is_extra = jnp.logical_and(row == 0, core == 0)
    sends_main = low == 0
    sends_extra = jnp.logical_and(low == 1, is_extra)

    def main_place(y, c, h):
        return fresh_main.at[y, c, h]

    def az_copy(step, dst, sem):
        return remote(
            fresh, dst, az_send_sem.at[step - 1], az_recv_sem.at[sem], device(core, row, at_z(step))
        )

    @pl.when(sends_main)
    def _():
        for step in range(1, 8):
            az_copy(step, main_place(row, core, half), half).start()
        local = pltpu.make_async_copy(fresh, main_place(row, core, half), local_sem.at[1])
        local.start()
        local.wait()

    @pl.when(sends_extra)
    def _():
        for step in range(1, 8):
            az_copy(step, fresh_extra.at[half], 2 + half).start()
        local = pltpu.make_async_copy(fresh, fresh_extra.at[half], local_sem.at[2])
        local.start()
        local.wait()

    for h in range(2):

        @pl.when(z != 4 * h)
        def _():
            az_copy(1, main_place(row, core, h), h).wait_recv()

    def ay_copy(y, step):
        return remote(
            fresh_main.at[y, core],
            fresh_main.at[y, core],
            ay_send_sem.at[step - 1],
            ay_recv_sem.at[step - 1],
            device(core, at_y(step), z),
        )

    def ac_copy(y, c):
        return remote(
            fresh_main.at[y, c],
            fresh_main.at[y, c],
            ac_send_sem.at[y],
            ac_recv_sem.at[y],
            device(1 - core, row, z),
        )

    for step in (2, 1, 3):
        ay_copy(row, step).start()
    ac_copy(row, core).start()

    def ey_copy(step):
        return remote(
            fresh_extra,
            fresh_extra,
            ay_send_sem.at[2 + step],
            ay_recv_sem.at[3],
            device(core, at_y(step), z),
        )

    def ec_copy():
        return remote(
            fresh_extra, fresh_extra, ac_send_sem.at[4], ac_recv_sem.at[4], device(1 - core, row, z)
        )

    @pl.when(is_extra)
    def _():
        for h in range(2):

            @pl.when(z != 4 * h + 1)
            def _():
                az_copy(1, fresh_extra.at[h], 2 + h).wait_recv()

        for step in range(1, 4):
            ey_copy(step).start()
        ec_copy().start()

    for step in (1, 3, 2):
        source = lax.rem(row - step + 4, 4)
        ay_copy(source, step).wait_recv()
        ac_copy(source, core).start()

    @pl.when(jnp.logical_and(row != 0, core == 0))
    def _():
        ey_copy(1).wait_recv()
        ec_copy().start()

    for step in range(4):
        ac_copy(at_y(step), 1 - core).wait_recv()

    @pl.when(core == 1)
    def _():
        ec_copy().wait_recv()

    for j, (block, wanted, own) in enumerate(takes):

        @pl.when(jnp.logical_and(wanted, jnp.logical_not(own)))
        def _():
            remote(
                fresh,
                fresh_second.at[j],
                b_send_sem.at[0],
                b_recv_sem.at[j],
                {"dp": lax.div(block, 2), "rollout": lax.rem(block, 2)},
            ).wait_recv()

    for chunk in range(16):
        core_copy(chunk).wait_send()
    for g in range(4):
        for step in range(1, 4):
            y_copy(g, step).wait_send()
    for step in range(1, 8):
        z_copy(step - 1, at_z(step), at_z(step)).wait_send()
    for q, (user, t, slot, wanted, own) in enumerate(sends):

        @pl.when(jnp.logical_and(wanted, jnp.logical_not(own)))
        def _():
            remote(
                fresh,
                fresh_second.at[slot],
                b_send_sem.at[q],
                b_recv_sem.at[slot],
                {"dp": user, "rollout": t},
            ).wait_send()

    @pl.when(jnp.logical_or(sends_main, sends_extra))
    def _():
        for step in range(1, 8):
            az_copy(step, fresh_extra.at[half], 0).wait_send()

    for step in range(1, 4):
        ay_copy(row, step).wait_send()
    for y in range(4):
        ac_copy(y, core).wait_send()

    @pl.when(is_extra)
    def _():
        for step in range(1, 4):
            ey_copy(step).wait_send()

    @pl.when(core == 0)
    def _():
        ec_copy().wait_send()

    grad_copy.wait()
    base_copy.wait()


def exchange(*operands):
    any_space = pl.BlockSpec(memory_space=pl.ANY)
    dma = pltpu.SemaphoreType.DMA
    return pl.pallas_call(
        exchange_kernel,
        out_shape=(
            jax.ShapeDtypeStruct((EXPERTS, INNER // 2, SPAN), BF16),
            jax.ShapeDtypeStruct((4, 2, 2, PAIR, 128), BF16),
            jax.ShapeDtypeStruct((2, PAIR, 128), BF16),
            jax.ShapeDtypeStruct((3, PAIR, 128), BF16),
            jax.ShapeDtypeStruct((PAIR, 128), F32),
        ),
        in_specs=[any_space] * len(operands),
        out_specs=(any_space,) * 5,
        scratch_shapes=[
            pltpu.VMEM((SLOTS, INNER), BF16),
            pltpu.VMEM((TOK, WIDE), BF16),
            pltpu.VMEM((ROWS, COLS), BF16),
            pltpu.VMEM((EXPERTS, CAP), jnp.int32),
            pltpu.VMEM((EXPERTS, CAP), F32),
            pltpu.VMEM((EXPERTS, 1), jnp.int32),
            pltpu.VMEM((3, SHARD, COLS), F32),
            pltpu.VMEM((EXPERTS, 2, TOK, CAP), BF16),
            pltpu.VMEM((SLOTS, COLS), BF16),
            pltpu.VMEM((ROWS, COLS), F32),
            pltpu.VMEM((16, PAIR, COLS), F32),
            pltpu.VMEM((4, 3, PAIR, COLS), BF16),
            pltpu.VMEM((4, 3, PAIR, COLS), BF16),
            pltpu.VMEM((8, PAIR, 128), F32),
            pltpu.VMEM((8, PAIR, 128), BF16),
            pltpu.VMEM((7, PAIR, 128), BF16),
            pltpu.VMEM((PAIR, 128), BF16),
            dma((13,)),
            dma((6,)),
            dma((2,)),
            dma((16,)),
            dma((16,)),
            dma((4, 3)),
            dma((4, 3)),
            dma((7,)),
            dma((7,)),
            dma((7,)),
            dma((4,)),
            dma((6,)),
            dma((4,)),
            dma((5,)),
            dma((5,)),
            dma((4,)),
            dma((3,)),
        ],
        compiler_params=pltpu.CompilerParams(
            collective_id=0, has_side_effects=True, vmem_limit_bytes=56 * 2**20
        ),
    )(*operands)


def merge_kernel(
    base_own,
    base_other,
    fresh_main,
    fresh_extra,
    fresh_second,
    grad_total,
    precise,
    mean,
    variance,
    merged,
    revised_out,
    first_out,
    second_out,
    wide,
    first,
    second,
    near,
):
    e = pl.program_id(0)
    dp = lax.axis_index("dp")
    half = lax.axis_index("rollout")

    @pl.when(e == 0)
    def _():
        for block in range(A_BLOCKS):
            if block < 16:
                folded = fresh_main[block // 4, (block // 2) % 2, block % 2]
            else:
                folded = fresh_extra[block - 16]
            wide[block * SHARD : (block + 1) * SHARD] = unfold(folded.astype(F32))
        first[...] = wide[:INNER].astype(BF16)
        for j in range(3):
            near[j * SHARD : (j + 1) * SHARD] = unfold(fresh_second[j].astype(F32))
        skip = INNER + SPAN * dp - lax.div(INNER + SPAN * dp, SHARD) * SHARD
        second[...] = near[pl.ds(pl.multiple_of(skip, 8), SPAN)].astype(BF16)
        revised, new_first, new_second = adamw_update(
            unfold(grad_total[...]), precise[...], mean[...], variance[...]
        )
        revised_out[...] = revised
        first_out[...] = new_first
        second_out[...] = new_second

    lanes = lax.broadcasted_iota(jnp.int32, (SPAN, COLS), 1)
    inside = jnp.logical_and(lanes >= e * 64, lanes < (e + 1) * 64)
    columns = jnp.where(inside, second[...].astype(F32), 0.0).astype(BF16)
    for part, tile in ((half, base_own), (1 - half, base_other)):
        rows = pl.ds(pl.multiple_of(part * (INNER // 2), 256), INNER // 2)
        product = lax.dot_general(
            first[rows], columns, (((1,), (1,)), ((), ())), preferred_element_type=F32
        )
        merged[0, rows] = (tile[0].astype(F32) + delta_multiplier * product).astype(BF16)


def merge(*operands):
    half_tile = pl.BlockSpec((1, INNER // 2, SPAN), lambda e: (e, 0, 0))

    def whole(shape):
        return pl.BlockSpec(shape, lambda e: (0,) * len(shape))

    shard = whole((SHARD, COLS))
    shard_type = jax.ShapeDtypeStruct((SHARD, COLS), F32)
    return pl.pallas_call(
        merge_kernel,
        grid=(EXPERTS,),
        out_shape=(
            jax.ShapeDtypeStruct((EXPERTS, INNER, SPAN), BF16),
            shard_type,
            shard_type,
            shard_type,
        ),
        in_specs=[
            half_tile,
            half_tile,
            whole((4, 2, 2, PAIR, 128)),
            whole((2, PAIR, 128)),
            whole((3, PAIR, 128)),
            whole((PAIR, 128)),
            shard,
            shard,
            shard,
        ],
        out_specs=(
            pl.BlockSpec((1, INNER, SPAN), lambda e: (e, 0, 0)),
            shard,
            shard,
            shard,
        ),
        scratch_shapes=[
            pltpu.VMEM((A_BLOCKS * SHARD, COLS), F32),
            pltpu.VMEM((INNER, COLS), BF16),
            pltpu.VMEM((SPAN, COLS), BF16),
            pltpu.VMEM((3 * SHARD, COLS), F32),
        ],
        compiler_params=pltpu.CompilerParams(vmem_limit_bytes=32 * 2**20),
    )(*operands)


def body(
    hidden,
    slot_token,
    gate,
    counts,
    cotangent,
    halfwidth_replica,
    precise_matrices,
    running_mean,
    running_variance,
    base,
):
    base_other, fresh_main, fresh_extra, fresh_second, grad_total = exchange(
        hidden,
        slot_token,
        gate,
        counts,
        cotangent,
        halfwidth_replica,
        precise_matrices,
        running_mean,
        running_variance,
        base,
    )
    return merge(
        base,
        base_other,
        fresh_main,
        fresh_extra,
        fresh_second,
        grad_total,
        precise_matrices,
        running_mean,
        running_variance,
    )


def solution(mesh):
    in_specs = (
        P("expert", ("dp", "rollout"), None),
        P("expert", ("dp", "rollout")),
        P("expert", ("dp", "rollout")),
        P("expert", ("dp", "rollout")),
        P(("dp", "rollout"), None),
        P(None, "expert"),
        P(("dp", "rollout"), "expert"),
        P(("dp", "rollout"), "expert"),
        P(("dp", "rollout"), "expert"),
        P("expert", "rollout", "dp"),
    )
    out_specs = (
        P("expert", None, "dp"),
        P(("dp", "rollout"), "expert"),
        P(("dp", "rollout"), "expert"),
        P(("dp", "rollout"), "expert"),
    )
    return jax.shard_map(body, mesh=mesh, in_specs=in_specs, out_specs=out_specs, check_vma=False)
```

```python
import functools

import jax
import jax.numpy as jnp
from jax import lax
from jax.experimental import pallas as pl
from jax.experimental.pallas import tpu as pltpu
from jax.sharding import PartitionSpec as P

STEP = 100

delta_multiplier = 2.0
beta_first = 0.9
beta_second = 0.95
learn_rate = 0.04
decay_rate = 0.01
adam_eps = 1e-08

MESH = pl.DeviceIdType.MESH
BF16 = jnp.bfloat16
F32 = jnp.float32

EXPERTS = 4
CAP = 320
SLOTS = EXPERTS * CAP
INNER = 1536
WIDE = 4096
TOK = 512
COLS = 256
ROWS = INNER + WIDE
SHARD = 88
PAIR = 2 * SHARD
TILE = 512
SPAN = 128
A_BLOCKS = 18
PIECES = 4
BASE_TURNS = (11, 0, 5)


def adamw_update(derivative_total, precise_matrices, running_mean, running_variance):
    new_first = beta_first * running_mean + (1.0 - beta_first) * derivative_total
    new_second = (
        beta_second * running_variance + (1.0 - beta_second) * derivative_total * derivative_total
    )
    first_hat = new_first / (1.0 - beta_first**STEP)
    second_hat = new_second / (1.0 - beta_second**STEP)
    revised_precise = precise_matrices - learn_rate * (
        first_hat / (jnp.sqrt(second_hat) + adam_eps) + decay_rate * precise_matrices
    )
    return (revised_precise, new_first, new_second)


def fold(block):
    return jnp.concatenate([block[:, :128], block[:, 128:]], axis=0)


def unfold(block):
    return jnp.concatenate([block[:SHARD], block[SHARD:]], axis=1)


def dot(lhs, rhs):
    return jnp.dot(lhs, rhs, preferred_element_type=F32)


def dot_t(lhs, rhs):
    return lax.dot_general(lhs, rhs, (((0,), (0,)), ((), ())), preferred_element_type=F32)


def split(value):
    high = value.astype(BF16)
    return high, (value - high.astype(F32)).astype(BF16)


def exchange_kernel(
    hidden,
    slot_token,
    gate,
    counts,
    cotangent,
    factors,
    precise,
    mean,
    variance,
    base,
    base_other,
    fresh_main,
    fresh_extra,
    fresh_second,
    grad_out,
    hid,
    cot,
    fac,
    tok_v,
    gate_v,
    counts_v,
    opt_v,
    select,
    slots_v,
    grad,
    from_core,
    y_send,
    y_recv,
    z_keep,
    z_send,
    z_recv,
    fresh,
    load_sem,
    local_sem,
    base_send_sem,
    base_recv_sem,
    core_send_sem,
    core_recv_sem,
    y_send_sem,
    y_recv_sem,
    z_send_sem,
    z_recv_sem,
    az_send_sem,
    az_recv_sem,
    ay_send_sem,
    ay_recv_sem,
    ac_send_sem,
    ac_recv_sem,
    b_send_sem,
    b_recv_sem,
):
    dp = lax.axis_index("dp")
    half = lax.axis_index("rollout")
    core = lax.rem(dp, 2)
    row = lax.rem(lax.div(dp, 2), 4)
    low = lax.div(dp, 8)
    z = half * 4 + low
    mine = dp * 2 + half

    def device(c, y, zz):
        return {"dp": lax.rem(zz, 4) * 8 + y * 2 + c, "rollout": lax.div(zz, 4)}

    def at_y(step):
        return lax.rem(row + step, 4)

    def at_z(step):
        return lax.rem(z + step, 8)

    def remote(src, dst, send, recv, target):
        return pltpu.make_async_remote_copy(
            src_ref=src,
            dst_ref=dst,
            send_sem=send,
            recv_sem=recv,
            device_id=target,
            device_id_type=MESH,
        )

    loads = []

    def load(src, dst):
        copy = pltpu.make_async_copy(src, dst, load_sem.at[len(loads)])
        copy.start()
        loads.append(copy)
        return copy

    load_c = load(cotangent, cot)
    load_b = load(factors.at[pl.ds(INNER, WIDE)], fac.at[pl.ds(INNER, WIDE)])
    load_small = [load(slot_token, tok_v), load(gate, gate_v), load(counts, counts_v)]
    load_h = [
        load(hidden.at[e], hid.at[pl.ds(e * CAP, CAP)]) for e in range(EXPERTS)
    ]
    load_a = load(factors.at[pl.ds(0, INNER)], fac.at[pl.ds(0, INNER)])
    load_o = [
        load(precise, opt_v.at[0]),
        load(mean, opt_v.at[1]),
        load(variance, opt_v.at[2]),
    ]

    sends = []
    first_row = mine * SHARD - INNER
    first_user = lax.div(jnp.maximum(first_row, 0), SPAN)
    last_user = lax.div(jnp.maximum(first_row + SHARD - 1, 0), SPAN)
    has_second = first_row + SHARD > 0
    for q, user in enumerate((first_user, last_user)):
        wanted = has_second if q == 0 else jnp.logical_and(has_second, last_user != first_user)
        slot = mine - lax.div(INNER + SPAN * user, SHARD)
        for t in range(2):
            own = jnp.logical_and(user == dp, half == t)
            sends.append((user, t, slot, wanted, own))
    first_block = lax.div(INNER + SPAN * dp, SHARD)
    takes = []
    for j in range(3):
        block = first_block + j
        wanted = block * SHARD < INNER + SPAN * dp + SPAN
        takes.append((block, wanted, block == mine))

    barrier = pltpu.get_barrier_semaphore()

    def greet(target):
        pl.semaphore_signal(barrier, inc=1, device_id=target, device_id_type=MESH)

    greet(device(1 - core, row, z))
    for step in range(1, 4):
        greet(device(core, at_y(step), z))
    for step in range(1, 8):
        greet(device(core, row, at_z(step)))
    for user, t, slot, wanted, own in sends:

        @pl.when(jnp.logical_and(wanted, jnp.logical_not(own)))
        def _():
            greet({"dp": user, "rollout": t})

    for block, wanted, own in takes:

        @pl.when(jnp.logical_and(wanted, jnp.logical_not(own)))
        def _():
            greet({"dp": lax.div(block, 2), "rollout": lax.rem(block, 2)})

    greeted = 11
    for wanted, own in [s[3:] for s in sends] + [t[1:] for t in takes]:
        greeted = greeted + jnp.where(jnp.logical_and(wanted, jnp.logical_not(own)), 1, 0)
    pl.semaphore_wait(barrier, greeted)

    def base_copy(piece):
        rows = INNER // 2 // PIECES
        place = (piece // PIECES, pl.ds(piece % PIECES * rows, rows))
        return remote(
            base.at[place],
            base_other.at[place],
            base_send_sem.at[piece],
            base_recv_sem.at[piece],
            device(core, row, at_z(4)),
        )

    def send_base(turn):
        first = sum(BASE_TURNS[:turn])
        for piece in range(first, first + BASE_TURNS[turn]):
            base_copy(piece).start()

    send_base(0)

    for copy in load_small:
        copy.wait()
    places = lax.broadcasted_iota(jnp.int32, (1, CAP), 1)
    tokens = lax.broadcasted_iota(jnp.int32, (TOK, CAP), 0)
    for e in range(EXPERTS):
        live_gate = jnp.where(places < counts_v[0, e], gate_v[e : e + 1], 0.0)
        gate_high = live_gate.astype(BF16).astype(F32)
        gate_low = live_gate - gate_high
        hit = tokens == tok_v[e : e + 1]
        for part, value in enumerate((gate_high, gate_low)):
            select[e, part] = jnp.where(hit, value, 0.0).astype(BF16)
    lanes = lax.broadcasted_iota(jnp.int32, (CAP, COLS), 1)
    load_c.wait()
    load_b.wait()
    back_high, back_low = split(dot(cot[...], fac[INNER:]))
    for e in range(EXPERTS):
        inside = jnp.logical_and(lanes >= e * 64, lanes < (e + 1) * 64)
        back = (
            dot_t(select[e, 0], back_high)
            + dot_t(select[e, 1], back_high)
            + dot_t(select[e, 0], back_low)
        )
        slots_v[e * CAP : (e + 1) * CAP] = jnp.where(inside, back, 0.0).astype(BF16)

    def core_copy(chunk):
        return remote(
            grad.at[pl.ds(pl.multiple_of(352 * chunk + PAIR * (1 - core), 8), PAIR)],
            from_core.at[chunk],
            core_send_sem.at[chunk],
            core_recv_sem.at[chunk],
            device(1 - core, row, z),
        )

    def own_rows(chunk):
        return grad[pl.ds(pl.multiple_of(352 * chunk + PAIR * core, 8), PAIR)]

    def y_copy(g, step):
        return remote(
            y_send.at[g, step - 1],
            y_recv.at[g, step - 1],
            y_send_sem.at[g, step - 1],
            y_recv_sem.at[g, step - 1],
            device(core, at_y(step), z),
        )

    def to_core(g):
        for chunk in range(4 * g, 4 * g + 4):
            core_copy(chunk).start()

    def to_y(g):
        for chunk in range(4 * g, 4 * g + 4):
            core_copy(chunk).wait_recv()
        for step in (2, 1, 3):
            chunk = 4 * g + at_y(step)
            y_send[g, step - 1] = (own_rows(chunk) + from_core[chunk]).astype(BF16)
            y_copy(g, step).start()

    for copy in load_h:
        copy.wait()
    for tile in range(3):
        grad[tile * TILE : (tile + 1) * TILE] = dot_t(
            hid[:, tile * TILE : (tile + 1) * TILE], slots_v[...]
        )
    to_core(0)

    load_a.wait()
    by_token = jnp.zeros((TOK, COLS), F32)
    for e in range(EXPERTS):
        down = dot(hid[e * CAP : (e + 1) * CAP], fac[:INNER])
        inside = jnp.logical_and(lanes >= e * 64, lanes < (e + 1) * 64)
        down = jnp.where(inside, down, 0.0).astype(BF16)
        by_token = by_token + dot(select[e, 0], down) + dot(select[e, 1], down)
    token_high, token_low = split(by_token)
    to_y(0)

    def second_tile(tile):
        lhs = cot[:, tile * TILE : (tile + 1) * TILE]
        grad[INNER + tile * TILE : INNER + (tile + 1) * TILE] = dot_t(lhs, token_high) + dot_t(
            lhs, token_low
        )

    for tile in range(0, 3):
        second_tile(tile)
    to_core(1)
    for tile in range(3, 6):
        second_tile(tile)
    to_core(2)
    to_y(1)
    for tile in range(6, 8):
        second_tile(tile)
    to_core(3)
    to_y(2)
    to_y(3)

    def z_copy(step_index, block, target):
        return remote(
            z_send.at[block],
            z_recv.at[step_index],
            z_send_sem.at[step_index],
            z_recv_sem.at[step_index],
            device(core, row, target),
        )

    def to_z(g):
        for step in range(1, 4):
            y_copy(g, step).wait_recv()
        chunk = 4 * g + row
        total = own_rows(chunk) + from_core[chunk]
        for step in range(3):
            total = total + y_recv[g, step].astype(F32)
        for h in range(2):
            target = 4 * h + g
            block = fold(total[h * SHARD : (h + 1) * SHARD])
            z_keep[target] = block
            z_send[target] = block.astype(BF16)
            distance = lax.rem(target - z + 8, 8)

            @pl.when(distance != 0)
            def _():
                z_copy(distance - 1, target, target).start()

    grad_copy = pltpu.make_async_copy(z_keep.at[8], grad_out, local_sem.at[5])

    def b_copy(q):
        user, t, slot = sends[q][:3]
        return remote(
            fresh,
            fresh_second.at[slot],
            b_send_sem.at[q],
            b_recv_sem.at[slot],
            {"dp": user, "rollout": t},
        )

    def update():
        derivative = z_keep[z]
        for step in range(1, 8):
            z_copy(step - 1, at_z(step), at_z(step)).wait_recv()
            derivative = derivative + z_recv[step - 1].astype(F32)
        derivative = delta_multiplier * derivative
        z_keep[8] = derivative
        revised, unused_first, unused_second = adamw_update(
            unfold(derivative), opt_v[0], opt_v[1], opt_v[2]
        )
        fresh[...] = fold(revised).astype(BF16)
        grad_copy.start()

    def send_second(q):
        user, t, slot, wanted, own = sends[q]

        @pl.when(jnp.logical_and(wanted, jnp.logical_not(own)))
        def _():
            b_copy(q).start()

        @pl.when(jnp.logical_and(wanted, own))
        def _():
            local = pltpu.make_async_copy(fresh, fresh_second.at[slot], local_sem.at[0])
            local.start()
            local.wait()

    is_extra = jnp.logical_and(row == 0, core == 0)
    sends_main = low == 0
    sends_extra = jnp.logical_and(low == 1, is_extra)

    def main_place(y, c, h):
        return fresh_main.at[y, c, h]

    def az_copy(step, dst, sem):
        return remote(
            fresh, dst, az_send_sem.at[step - 1], az_recv_sem.at[sem], device(core, row, at_z(step))
        )

    for copy in load_o:
        copy.wait()
    for g in range(4):
        to_z(g)
    send_base(1)
    update()

    @pl.when(low == 0)
    def _():
        for step in range(1, 8):
            az_copy(step, main_place(row, core, half), half).start()
        local = pltpu.make_async_copy(fresh, main_place(row, core, half), local_sem.at[1])
        local.start()
        local.wait()

    @pl.when(sends_extra)
    def _():
        for step in range(1, 8):
            az_copy(step, fresh_extra.at[half], 2 + half).start()
        local = pltpu.make_async_copy(fresh, fresh_extra.at[half], local_sem.at[2])
        local.start()
        local.wait()

    for q in range(len(sends)):
        send_second(q)

    send_base(2)

    for h in range(2):

        @pl.when(z != 4 * h)
        def _():
            az_copy(1, main_place(row, core, h), h).wait_recv()

    def ay_copy(y, step):
        return remote(
            fresh_main.at[y, core],
            fresh_main.at[y, core],
            ay_send_sem.at[step - 1],
            ay_recv_sem.at[step - 1],
            device(core, at_y(step), z),
        )

    def ac_copy(y, c):
        return remote(
            fresh_main.at[y, c],
            fresh_main.at[y, c],
            ac_send_sem.at[y],
            ac_recv_sem.at[y],
            device(1 - core, row, z),
        )

    for step in (2, 1, 3):
        ay_copy(row, step).start()
    ac_copy(row, core).start()

    def ey_copy(step):
        return remote(
            fresh_extra,
            fresh_extra,
            ay_send_sem.at[2 + step],
            ay_recv_sem.at[3],
            device(core, at_y(step), z),
        )

    def ec_copy():
        return remote(
            fresh_extra, fresh_extra, ac_send_sem.at[4], ac_recv_sem.at[4], device(1 - core, row, z)
        )

    @pl.when(is_extra)
    def _():
        for h in range(2):

            @pl.when(z != 4 * h + 1)
            def _():
                az_copy(1, fresh_extra.at[h], 2 + h).wait_recv()

        for step in range(1, 4):
            ey_copy(step).start()
        ec_copy().start()

    for step in (1, 3, 2):
        source = lax.rem(row - step + 4, 4)
        ay_copy(source, step).wait_recv()
        ac_copy(source, core).start()

    @pl.when(jnp.logical_and(row != 0, core == 0))
    def _():
        ey_copy(1).wait_recv()
        ec_copy().start()

    for step in range(4):
        ac_copy(at_y(step), 1 - core).wait_recv()

    @pl.when(core == 1)
    def _():
        ec_copy().wait_recv()

    for j, (block, wanted, own) in enumerate(takes):

        @pl.when(jnp.logical_and(wanted, jnp.logical_not(own)))
        def _():
            remote(
                fresh,
                fresh_second.at[j],
                b_send_sem.at[0],
                b_recv_sem.at[j],
                {"dp": lax.div(block, 2), "rollout": lax.rem(block, 2)},
            ).wait_recv()

    for chunk in range(16):
        core_copy(chunk).wait_send()
    for g in range(4):
        for step in range(1, 4):
            y_copy(g, step).wait_send()
    for step in range(1, 8):
        z_copy(step - 1, at_z(step), at_z(step)).wait_send()
    for q, (user, t, slot, wanted, own) in enumerate(sends):

        @pl.when(jnp.logical_and(wanted, jnp.logical_not(own)))
        def _():
            b_copy(q).wait_send()

    @pl.when(jnp.logical_or(sends_main, sends_extra))
    def _():
        for step in range(1, 8):
            az_copy(step, fresh_extra.at[half], 0).wait_send()

    for step in range(1, 4):
        ay_copy(row, step).wait_send()
    for y in range(4):
        ac_copy(y, core).wait_send()

    @pl.when(is_extra)
    def _():
        for step in range(1, 4):
            ey_copy(step).wait_send()

    @pl.when(core == 0)
    def _():
        ec_copy().wait_send()

    grad_copy.wait()
    for piece in range(EXPERTS * PIECES):
        base_copy(piece).wait()


def exchange(*operands):
    any_space = pl.BlockSpec(memory_space=pl.ANY)
    dma = pltpu.SemaphoreType.DMA
    return pl.pallas_call(
        exchange_kernel,
        out_shape=(
            jax.ShapeDtypeStruct((EXPERTS, INNER // 2, SPAN), BF16),
            jax.ShapeDtypeStruct((4, 2, 2, PAIR, 128), BF16),
            jax.ShapeDtypeStruct((2, PAIR, 128), BF16),
            jax.ShapeDtypeStruct((3, PAIR, 128), BF16),
            jax.ShapeDtypeStruct((PAIR, 128), F32),
        ),
        in_specs=[any_space] * len(operands),
        out_specs=(any_space,) * 5,
        scratch_shapes=[
            pltpu.VMEM((SLOTS, INNER), BF16),
            pltpu.VMEM((TOK, WIDE), BF16),
            pltpu.VMEM((ROWS, COLS), BF16),
            pltpu.VMEM((EXPERTS, CAP), jnp.int32),
            pltpu.VMEM((EXPERTS, CAP), F32),
            pltpu.SMEM((1, EXPERTS), jnp.int32),
            pltpu.VMEM((3, SHARD, COLS), F32),
            pltpu.VMEM((EXPERTS, 2, TOK, CAP), BF16),
            pltpu.VMEM((SLOTS, COLS), BF16),
            pltpu.VMEM((ROWS, COLS), F32),
            pltpu.VMEM((16, PAIR, COLS), F32),
            pltpu.VMEM((4, 3, PAIR, COLS), BF16),
            pltpu.VMEM((4, 3, PAIR, COLS), BF16),
            pltpu.VMEM((9, PAIR, 128), F32),
            pltpu.VMEM((8, PAIR, 128), BF16),
            pltpu.VMEM((7, PAIR, 128), BF16),
            pltpu.VMEM((PAIR, 128), BF16),
            dma((13,)),
            dma((6,)),
            dma((EXPERTS * PIECES,)),
            dma((EXPERTS * PIECES,)),
            dma((16,)),
            dma((16,)),
            dma((4, 3)),
            dma((4, 3)),
            dma((7,)),
            dma((7,)),
            dma((7,)),
            dma((4,)),
            dma((6,)),
            dma((4,)),
            dma((5,)),
            dma((5,)),
            dma((4,)),
            dma((3,)),
        ],
        compiler_params=pltpu.CompilerParams(
            collective_id=0, has_side_effects=True, vmem_limit_bytes=56 * 2**20
        ),
    )(*operands)


def merge_kernel(
    base_own,
    base_other,
    fresh_main,
    fresh_extra,
    fresh_second,
    grad_total,
    precise,
    mean,
    variance,
    merged,
    revised_out,
    first_out,
    second_out,
    wide,
    first,
    second,
    near,
):
    e = pl.program_id(0)
    dp = lax.axis_index("dp")
    half = lax.axis_index("rollout")

    @pl.when(e == 0)
    def _():
        for block in range(A_BLOCKS):
            if block < 16:
                folded = fresh_main[block // 4, (block // 2) % 2, block % 2]
            else:
                folded = fresh_extra[block - 16]
            wide[block * SHARD : (block + 1) * SHARD] = unfold(folded.astype(F32))
        first[...] = wide[:INNER].astype(BF16)
        for j in range(3):
            near[j * SHARD : (j + 1) * SHARD] = unfold(fresh_second[j].astype(F32))
        skip = INNER + SPAN * dp - lax.div(INNER + SPAN * dp, SHARD) * SHARD
        second[...] = near[pl.ds(pl.multiple_of(skip, 8), SPAN)].astype(BF16)
        revised, new_first, new_second = adamw_update(
            unfold(grad_total[...]), precise[...], mean[...], variance[...]
        )
        revised_out[...] = revised
        first_out[...] = new_first
        second_out[...] = new_second

    lanes = lax.broadcasted_iota(jnp.int32, (SPAN, COLS), 1)
    inside = jnp.logical_and(lanes >= e * 64, lanes < (e + 1) * 64)
    columns = jnp.where(inside, second[...].astype(F32), 0.0).astype(BF16)
    for part, tile in ((half, base_own), (1 - half, base_other)):
        rows = pl.ds(pl.multiple_of(part * (INNER // 2), 256), INNER // 2)
        product = lax.dot_general(
            first[rows], columns, (((1,), (1,)), ((), ())), preferred_element_type=F32
        )
        merged[0, rows] = (tile[0].astype(F32) + delta_multiplier * product).astype(BF16)


def merge(*operands):
    half_tile = pl.BlockSpec((1, INNER // 2, SPAN), lambda e: (e, 0, 0))

    def whole(shape):
        return pl.BlockSpec(shape, lambda e: (0,) * len(shape))

    shard = whole((SHARD, COLS))
    shard_type = jax.ShapeDtypeStruct((SHARD, COLS), F32)
    return pl.pallas_call(
        merge_kernel,
        grid=(EXPERTS,),
        out_shape=(
            jax.ShapeDtypeStruct((EXPERTS, INNER, SPAN), BF16),
            shard_type,
            shard_type,
            shard_type,
        ),
        in_specs=[
            half_tile,
            half_tile,
            whole((4, 2, 2, PAIR, 128)),
            whole((2, PAIR, 128)),
            whole((3, PAIR, 128)),
            whole((PAIR, 128)),
            shard,
            shard,
            shard,
        ],
        out_specs=(
            pl.BlockSpec((1, INNER, SPAN), lambda e: (e, 0, 0)),
            shard,
            shard,
            shard,
        ),
        scratch_shapes=[
            pltpu.VMEM((A_BLOCKS * SHARD, COLS), F32),
            pltpu.VMEM((INNER, COLS), BF16),
            pltpu.VMEM((SPAN, COLS), BF16),
            pltpu.VMEM((3 * SHARD, COLS), F32),
        ],
        compiler_params=pltpu.CompilerParams(vmem_limit_bytes=56 * 2**20),
    )(*operands)


def body(
    hidden,
    slot_token,
    gate,
    counts,
    cotangent,
    halfwidth_replica,
    precise_matrices,
    running_mean,
    running_variance,
    base,
):
    base_other, fresh_main, fresh_extra, fresh_second, grad_total = exchange(
        hidden,
        slot_token,
        gate,
        counts.reshape(1, EXPERTS),
        cotangent,
        halfwidth_replica,
        precise_matrices,
        running_mean,
        running_variance,
        base,
    )
    return merge(
        base,
        base_other,
        fresh_main,
        fresh_extra,
        fresh_second,
        grad_total,
        precise_matrices,
        running_mean,
        running_variance,
    )


def solution(mesh):
    in_specs = (
        P("expert", ("dp", "rollout"), None),
        P("expert", ("dp", "rollout")),
        P("expert", ("dp", "rollout")),
        P("expert", ("dp", "rollout")),
        P(("dp", "rollout"), None),
        P(None, "expert"),
        P(("dp", "rollout"), "expert"),
        P(("dp", "rollout"), "expert"),
        P(("dp", "rollout"), "expert"),
        P("expert", "rollout", "dp"),
    )
    out_specs = (
        P("expert", None, "dp"),
        P(("dp", "rollout"), "expert"),
        P(("dp", "rollout"), "expert"),
        P(("dp", "rollout"), "expert"),
    )
    return jax.shard_map(body, mesh=mesh, in_specs=in_specs, out_specs=out_specs, check_vma=False)
```

```python
import functools

import jax
import jax.numpy as jnp
from jax import lax
from jax.experimental import pallas as pl
from jax.experimental.pallas import tpu as pltpu
from jax.sharding import PartitionSpec as P

STEP = 100

delta_multiplier = 2.0
beta_first = 0.9
beta_second = 0.95
learn_rate = 0.04
decay_rate = 0.01
adam_eps = 1e-08

MESH = pl.DeviceIdType.MESH
BF16 = jnp.bfloat16
F32 = jnp.float32

EXPERTS = 4
CAP = 320
SLOTS = EXPERTS * CAP
INNER = 1536
WIDE = 4096
TOK = 512
COLS = 256
ROWS = INNER + WIDE
SHARD = 88
PAIR = 2 * SHARD
TILE = 512
SPAN = 128
A_BLOCKS = 18
PIECES = 4
BASE_TURNS = (11, 0, 5)


def adamw_update(derivative_total, precise_matrices, running_mean, running_variance):
    new_first = beta_first * running_mean + (1.0 - beta_first) * derivative_total
    new_second = (
        beta_second * running_variance + (1.0 - beta_second) * derivative_total * derivative_total
    )
    first_hat = new_first / (1.0 - beta_first**STEP)
    second_hat = new_second / (1.0 - beta_second**STEP)
    revised_precise = precise_matrices - learn_rate * (
        first_hat / (jnp.sqrt(second_hat) + adam_eps) + decay_rate * precise_matrices
    )
    return (revised_precise, new_first, new_second)


def fold(block):
    return jnp.concatenate([block[:, :128], block[:, 128:]], axis=0)


def unfold(block):
    return jnp.concatenate([block[:SHARD], block[SHARD:]], axis=1)


def dot(lhs, rhs):
    return jnp.dot(lhs, rhs, preferred_element_type=F32)


def dot_t(lhs, rhs):
    return lax.dot_general(lhs, rhs, (((0,), (0,)), ((), ())), preferred_element_type=F32)


def split(value):
    high = value.astype(BF16)
    return high, (value - high.astype(F32)).astype(BF16)


def exchange_kernel(
    hidden,
    slot_token,
    gate,
    counts,
    cotangent,
    factors,
    precise,
    mean,
    variance,
    base,
    base_other,
    fresh_main,
    fresh_extra,
    fresh_second,
    grad_out,
    hid,
    cot,
    fac,
    tok_v,
    gate_v,
    counts_v,
    opt_v,
    select,
    slots_v,
    grad,
    from_core,
    y_send,
    y_recv,
    z_keep,
    z_send,
    z_recv,
    fresh,
    load_sem,
    local_sem,
    base_send_sem,
    base_recv_sem,
    core_send_sem,
    core_recv_sem,
    y_send_sem,
    y_recv_sem,
    z_send_sem,
    z_recv_sem,
    az_send_sem,
    az_recv_sem,
    ay_send_sem,
    ay_recv_sem,
    ac_send_sem,
    ac_recv_sem,
    b_send_sem,
    b_recv_sem,
):
    dp = lax.axis_index("dp")
    half = lax.axis_index("rollout")
    core = lax.rem(dp, 2)
    row = lax.rem(lax.div(dp, 2), 4)
    low = lax.div(dp, 8)
    z = half * 4 + low
    mine = dp * 2 + half

    def device(c, y, zz):
        return {"dp": lax.rem(zz, 4) * 8 + y * 2 + c, "rollout": lax.div(zz, 4)}

    def at_y(step):
        return lax.rem(row + step, 4)

    def at_z(step):
        return lax.rem(z + step, 8)

    def remote(src, dst, send, recv, target):
        return pltpu.make_async_remote_copy(
            src_ref=src,
            dst_ref=dst,
            send_sem=send,
            recv_sem=recv,
            device_id=target,
            device_id_type=MESH,
        )

    loads = []

    def load(src, dst):
        copy = pltpu.make_async_copy(src, dst, load_sem.at[len(loads)])
        copy.start()
        loads.append(copy)
        return copy

    load_c = load(cotangent, cot)
    load_b = load(factors.at[pl.ds(INNER, WIDE)], fac.at[pl.ds(INNER, WIDE)])
    load_small = [load(slot_token, tok_v), load(gate, gate_v), load(counts, counts_v)]
    load_h = [
        load(hidden.at[e], hid.at[pl.ds(e * CAP, CAP)]) for e in range(EXPERTS)
    ]
    load_a = load(factors.at[pl.ds(0, INNER)], fac.at[pl.ds(0, INNER)])
    load_o = [
        load(precise, opt_v.at[0]),
        load(mean, opt_v.at[1]),
        load(variance, opt_v.at[2]),
    ]

    sends = []
    first_row = mine * SHARD - INNER
    first_user = lax.div(jnp.maximum(first_row, 0), SPAN)
    last_user = lax.div(jnp.maximum(first_row + SHARD - 1, 0), SPAN)
    has_second = first_row + SHARD > 0
    for q, user in enumerate((first_user, last_user)):
        wanted = has_second if q == 0 else jnp.logical_and(has_second, last_user != first_user)
        slot = mine - lax.div(INNER + SPAN * user, SHARD)
        for t in range(2):
            own = jnp.logical_and(user == dp, half == t)
            sends.append((user, t, slot, wanted, own))
    first_block = lax.div(INNER + SPAN * dp, SHARD)
    takes = []
    for j in range(3):
        block = first_block + j
        wanted = block * SHARD < INNER + SPAN * dp + SPAN
        takes.append((block, wanted, block == mine))

    barrier = pltpu.get_barrier_semaphore()

    def greet(target):
        pl.semaphore_signal(barrier, inc=1, device_id=target, device_id_type=MESH)

    greet(device(1 - core, row, z))
    for step in range(1, 4):
        greet(device(core, at_y(step), z))
    for step in range(1, 8):
        greet(device(core, row, at_z(step)))
    for user, t, slot, wanted, own in sends:

        @pl.when(jnp.logical_and(wanted, jnp.logical_not(own)))
        def _():
            greet({"dp": user, "rollout": t})

    for block, wanted, own in takes:

        @pl.when(jnp.logical_and(wanted, jnp.logical_not(own)))
        def _():
            greet({"dp": lax.div(block, 2), "rollout": lax.rem(block, 2)})

    greeted = 11
    for wanted, own in [s[3:] for s in sends] + [t[1:] for t in takes]:
        greeted = greeted + jnp.where(jnp.logical_and(wanted, jnp.logical_not(own)), 1, 0)
    pl.semaphore_wait(barrier, greeted)

    def base_copy(piece):
        rows = INNER // 2 // PIECES
        place = (piece // PIECES, pl.ds(piece % PIECES * rows, rows))
        return remote(
            base.at[place],
            base_other.at[place],
            base_send_sem.at[piece],
            base_recv_sem.at[piece],
            device(core, row, at_z(4)),
        )

    def send_base(turn):
        first = sum(BASE_TURNS[:turn])
        for piece in range(first, first + BASE_TURNS[turn]):
            base_copy(piece).start()

    send_base(0)

    for copy in load_small:
        copy.wait()
    places = lax.broadcasted_iota(jnp.int32, (1, CAP), 1)
    tokens = lax.broadcasted_iota(jnp.int32, (TOK, CAP), 0)
    for e in range(EXPERTS):
        live_gate = jnp.where(places < counts_v[0, e], gate_v[e : e + 1], 0.0)
        gate_high = live_gate.astype(BF16).astype(F32)
        gate_low = live_gate - gate_high
        hit = tokens == tok_v[e : e + 1]
        for part, value in enumerate((gate_high, gate_low)):
            select[e, part] = jnp.where(hit, value, 0.0).astype(BF16)
    lanes = lax.broadcasted_iota(jnp.int32, (CAP, COLS), 1)
    load_c.wait()
    load_b.wait()
    back_high, back_low = split(dot(cot[...], fac[INNER:]))
    for e in range(EXPERTS):
        inside = jnp.logical_and(lanes >= e * 64, lanes < (e + 1) * 64)
        back = (
            dot_t(select[e, 0], back_high)
            + dot_t(select[e, 1], back_high)
            + dot_t(select[e, 0], back_low)
        )
        slots_v[e * CAP : (e + 1) * CAP] = jnp.where(inside, back, 0.0).astype(BF16)

    def core_copy(chunk):
        return remote(
            grad.at[pl.ds(pl.multiple_of(352 * chunk + PAIR * (1 - core), 8), PAIR)],
            from_core.at[chunk],
            core_send_sem.at[chunk],
            core_recv_sem.at[chunk],
            device(1 - core, row, z),
        )

    def own_rows(chunk):
        return grad[pl.ds(pl.multiple_of(352 * chunk + PAIR * core, 8), PAIR)]

    side = 1 - 2 * core

    def y_copy(g, slot):
        way = -side if slot == 1 else side
        return remote(
            y_send.at[g, slot],
            y_recv.at[g, slot],
            y_send_sem.at[g, slot],
            y_recv_sem.at[g, slot],
            device(core, at_y(way + 4), z),
        )

    def to_core(g):
        for chunk in range(4 * g, 4 * g + 4):
            core_copy(chunk).start()

    def core_sum(g, step):
        chunk = 4 * g + at_y(step)
        return own_rows(chunk) + from_core[chunk]

    def to_y(g):
        for chunk in range(4 * g, 4 * g + 4):
            core_copy(chunk).wait_recv()
        for slot, step in ((0, 2), (1, 4 - side)):
            y_send[g, slot] = core_sum(g, step).astype(BF16)
            y_copy(g, slot).start()

    def on_along_y(g):
        y_copy(g, 0).wait_recv()
        y_send[g, 2] = (core_sum(g, 4 + side) + y_recv[g, 0].astype(F32)).astype(BF16)
        y_copy(g, 2).start()

    for copy in load_h:
        copy.wait()
    for tile in range(3):
        grad[tile * TILE : (tile + 1) * TILE] = dot_t(
            hid[:, tile * TILE : (tile + 1) * TILE], slots_v[...]
        )
    to_core(0)

    load_a.wait()
    by_token = jnp.zeros((TOK, COLS), F32)
    for e in range(EXPERTS):
        down = dot(hid[e * CAP : (e + 1) * CAP], fac[:INNER])
        inside = jnp.logical_and(lanes >= e * 64, lanes < (e + 1) * 64)
        down = jnp.where(inside, down, 0.0).astype(BF16)
        by_token = by_token + dot(select[e, 0], down) + dot(select[e, 1], down)
    token_high, token_low = split(by_token)
    to_y(0)

    def second_tile(tile):
        lhs = cot[:, tile * TILE : (tile + 1) * TILE]
        grad[INNER + tile * TILE : INNER + (tile + 1) * TILE] = dot_t(lhs, token_high) + dot_t(
            lhs, token_low
        )

    for tile in range(0, 3):
        second_tile(tile)
    to_core(1)
    for tile in range(3, 6):
        second_tile(tile)
    to_core(2)
    to_y(1)
    on_along_y(0)
    for tile in range(6, 8):
        second_tile(tile)
    to_core(3)
    to_y(2)
    on_along_y(1)
    to_y(3)
    on_along_y(2)
    on_along_y(3)

    def z_copy(step_index, block, target):
        return remote(
            z_send.at[block],
            z_recv.at[step_index],
            z_send_sem.at[step_index],
            z_recv_sem.at[step_index],
            device(core, row, target),
        )

    def to_z(g):
        total = core_sum(g, 0)
        for slot in (1, 2):
            y_copy(g, slot).wait_recv()
            total = total + y_recv[g, slot].astype(F32)
        for h in range(2):
            target = 4 * h + g
            block = fold(total[h * SHARD : (h + 1) * SHARD])
            z_keep[target] = block
            z_send[target] = block.astype(BF16)
            distance = lax.rem(target - z + 8, 8)

            @pl.when(distance != 0)
            def _():
                z_copy(distance - 1, target, target).start()

    grad_copy = pltpu.make_async_copy(z_keep.at[8], grad_out, local_sem.at[5])

    def b_copy(q):
        user, t, slot = sends[q][:3]
        return remote(
            fresh,
            fresh_second.at[slot],
            b_send_sem.at[q],
            b_recv_sem.at[slot],
            {"dp": user, "rollout": t},
        )

    def update():
        derivative = z_keep[z]
        for step in range(1, 8):
            z_copy(step - 1, at_z(step), at_z(step)).wait_recv()
            derivative = derivative + z_recv[step - 1].astype(F32)
        derivative = delta_multiplier * derivative
        z_keep[8] = derivative
        revised, unused_first, unused_second = adamw_update(
            unfold(derivative), opt_v[0], opt_v[1], opt_v[2]
        )
        fresh[...] = fold(revised).astype(BF16)
        grad_copy.start()

    def send_second(q):
        user, t, slot, wanted, own = sends[q]

        @pl.when(jnp.logical_and(wanted, jnp.logical_not(own)))
        def _():
            b_copy(q).start()

        @pl.when(jnp.logical_and(wanted, own))
        def _():
            local = pltpu.make_async_copy(fresh, fresh_second.at[slot], local_sem.at[0])
            local.start()
            local.wait()

    is_extra = jnp.logical_and(row == 0, core == 0)
    sends_main = low == 0
    sends_extra = jnp.logical_and(low == 1, is_extra)

    def main_place(y, c, h):
        return fresh_main.at[y, c, h]

    def az_copy(step, dst, sem):
        return remote(
            fresh, dst, az_send_sem.at[step - 1], az_recv_sem.at[sem], device(core, row, at_z(step))
        )

    for copy in load_o:
        copy.wait()
    for g in range(4):
        to_z(g)
    send_base(1)
    update()

    @pl.when(low == 0)
    def _():
        for step in range(1, 8):
            az_copy(step, main_place(row, core, half), half).start()
        local = pltpu.make_async_copy(fresh, main_place(row, core, half), local_sem.at[1])
        local.start()
        local.wait()

    @pl.when(sends_extra)
    def _():
        for step in range(1, 8):
            az_copy(step, fresh_extra.at[half], 2 + half).start()
        local = pltpu.make_async_copy(fresh, fresh_extra.at[half], local_sem.at[2])
        local.start()
        local.wait()

    for q in range(len(sends)):
        send_second(q)

    send_base(2)

    for h in range(2):

        @pl.when(z != 4 * h)
        def _():
            az_copy(1, main_place(row, core, h), h).wait_recv()

    def ay_copy(y, step):
        return remote(
            fresh_main.at[y, core],
            fresh_main.at[y, core],
            ay_send_sem.at[step - 1],
            ay_recv_sem.at[step - 1],
            device(core, at_y(step), z),
        )

    def ac_copy(y, c):
        return remote(
            fresh_main.at[y, c],
            fresh_main.at[y, c],
            ac_send_sem.at[y],
            ac_recv_sem.at[y],
            device(1 - core, row, z),
        )

    for step in (2, 1, 3):
        ay_copy(row, step).start()
    ac_copy(row, core).start()

    def ey_copy(step):
        return remote(
            fresh_extra,
            fresh_extra,
            ay_send_sem.at[2 + step],
            ay_recv_sem.at[3],
            device(core, at_y(step), z),
        )

    def ec_copy():
        return remote(
            fresh_extra, fresh_extra, ac_send_sem.at[4], ac_recv_sem.at[4], device(1 - core, row, z)
        )

    @pl.when(is_extra)
    def _():
        for h in range(2):

            @pl.when(z != 4 * h + 1)
            def _():
                az_copy(1, fresh_extra.at[h], 2 + h).wait_recv()

        for step in range(1, 4):
            ey_copy(step).start()
        ec_copy().start()

    for step in (1, 3, 2):
        source = lax.rem(row - step + 4, 4)
        ay_copy(source, step).wait_recv()
        ac_copy(source, core).start()

    @pl.when(jnp.logical_and(row != 0, core == 0))
    def _():
        ey_copy(1).wait_recv()
        ec_copy().start()

    for step in range(4):
        ac_copy(at_y(step), 1 - core).wait_recv()

    @pl.when(core == 1)
    def _():
        ec_copy().wait_recv()

    for j, (block, wanted, own) in enumerate(takes):

        @pl.when(jnp.logical_and(wanted, jnp.logical_not(own)))
        def _():
            remote(
                fresh,
                fresh_second.at[j],
                b_send_sem.at[0],
                b_recv_sem.at[j],
                {"dp": lax.div(block, 2), "rollout": lax.rem(block, 2)},
            ).wait_recv()

    for chunk in range(16):
        core_copy(chunk).wait_send()
    for g in range(4):
        for slot in range(3):
            y_copy(g, slot).wait_send()
    for step in range(1, 8):
        z_copy(step - 1, at_z(step), at_z(step)).wait_send()
    for q, (user, t, slot, wanted, own) in enumerate(sends):

        @pl.when(jnp.logical_and(wanted, jnp.logical_not(own)))
        def _():
            b_copy(q).wait_send()

    @pl.when(jnp.logical_or(sends_main, sends_extra))
    def _():
        for step in range(1, 8):
            az_copy(step, fresh_extra.at[half], 0).wait_send()

    for step in range(1, 4):
        ay_copy(row, step).wait_send()
    for y in range(4):
        ac_copy(y, core).wait_send()

    @pl.when(is_extra)
    def _():
        for step in range(1, 4):
            ey_copy(step).wait_send()

    @pl.when(core == 0)
    def _():
        ec_copy().wait_send()

    grad_copy.wait()
    for piece in range(EXPERTS * PIECES):
        base_copy(piece).wait()


def exchange(*operands):
    any_space = pl.BlockSpec(memory_space=pl.ANY)
    dma = pltpu.SemaphoreType.DMA
    return pl.pallas_call(
        exchange_kernel,
        out_shape=(
            pltpu.VMEM((EXPERTS, INNER // 2, SPAN), BF16),
            pltpu.VMEM((4, 2, 2, PAIR, 128), BF16),
            pltpu.VMEM((2, PAIR, 128), BF16),
            pltpu.VMEM((3, PAIR, 128), BF16),
            pltpu.VMEM((PAIR, 128), F32),
        ),
        in_specs=[any_space] * len(operands),
        out_specs=(any_space,) * 5,
        scratch_shapes=[
            pltpu.VMEM((SLOTS, INNER), BF16),
            pltpu.VMEM((TOK, WIDE), BF16),
            pltpu.VMEM((ROWS, COLS), BF16),
            pltpu.VMEM((EXPERTS, CAP), jnp.int32),
            pltpu.VMEM((EXPERTS, CAP), F32),
            pltpu.SMEM((1, EXPERTS), jnp.int32),
            pltpu.VMEM((3, SHARD, COLS), F32),
            pltpu.VMEM((EXPERTS, 2, TOK, CAP), BF16),
            pltpu.VMEM((SLOTS, COLS), BF16),
            pltpu.VMEM((ROWS, COLS), F32),
            pltpu.VMEM((16, PAIR, COLS), F32),
            pltpu.VMEM((4, 3, PAIR, COLS), BF16),
            pltpu.VMEM((4, 3, PAIR, COLS), BF16),
            pltpu.VMEM((9, PAIR, 128), F32),
            pltpu.VMEM((8, PAIR, 128), BF16),
            pltpu.VMEM((7, PAIR, 128), BF16),
            pltpu.VMEM((PAIR, 128), BF16),
            dma((13,)),
            dma((6,)),
            dma((EXPERTS * PIECES,)),
            dma((EXPERTS * PIECES,)),
            dma((16,)),
            dma((16,)),
            dma((4, 3)),
            dma((4, 3)),
            dma((7,)),
            dma((7,)),
            dma((7,)),
            dma((4,)),
            dma((6,)),
            dma((4,)),
            dma((5,)),
            dma((5,)),
            dma((4,)),
            dma((3,)),
        ],
        compiler_params=pltpu.CompilerParams(
            collective_id=0, has_side_effects=True, vmem_limit_bytes=60 * 2**20
        ),
    )(*operands)


def merge_kernel(
    base_own,
    base_other,
    fresh_main,
    fresh_extra,
    fresh_second,
    grad_total,
    precise,
    mean,
    variance,
    merged,
    revised_out,
    first_out,
    second_out,
    wide,
    first,
    second,
    near,
):
    e = pl.program_id(0)
    dp = lax.axis_index("dp")
    half = lax.axis_index("rollout")

    @pl.when(e == 0)
    def _():
        for block in range(A_BLOCKS):
            if block < 16:
                folded = fresh_main[block // 4, (block // 2) % 2, block % 2]
            else:
                folded = fresh_extra[block - 16]
            wide[block * SHARD : (block + 1) * SHARD] = unfold(folded.astype(F32))
        first[...] = wide[:INNER].astype(BF16)
        for j in range(3):
            near[j * SHARD : (j + 1) * SHARD] = unfold(fresh_second[j].astype(F32))
        skip = INNER + SPAN * dp - lax.div(INNER + SPAN * dp, SHARD) * SHARD
        second[...] = near[pl.ds(pl.multiple_of(skip, 8), SPAN)].astype(BF16)
        revised, new_first, new_second = adamw_update(
            unfold(grad_total[...]), precise[...], mean[...], variance[...]
        )
        revised_out[...] = revised
        first_out[...] = new_first
        second_out[...] = new_second

    lanes = lax.broadcasted_iota(jnp.int32, (SPAN, COLS), 1)
    inside = jnp.logical_and(lanes >= e * 64, lanes < (e + 1) * 64)
    columns = jnp.where(inside, second[...].astype(F32), 0.0).astype(BF16)
    for part, tile in ((half, base_own), (1 - half, base_other)):
        rows = pl.ds(pl.multiple_of(part * (INNER // 2), 256), INNER // 2)
        product = lax.dot_general(
            first[rows], columns, (((1,), (1,)), ((), ())), preferred_element_type=F32
        )
        merged[0, rows] = (tile[0].astype(F32) + delta_multiplier * product).astype(BF16)


def merge(*operands):
    half_tile = pl.BlockSpec((1, INNER // 2, SPAN), lambda e: (e, 0, 0))

    def whole(shape):
        return pl.BlockSpec(shape, lambda e: (0,) * len(shape))

    shard = whole((SHARD, COLS))
    shard_type = jax.ShapeDtypeStruct((SHARD, COLS), F32)
    return pl.pallas_call(
        merge_kernel,
        grid=(EXPERTS,),
        out_shape=(
            jax.ShapeDtypeStruct((EXPERTS, INNER, SPAN), BF16),
            shard_type,
            shard_type,
            shard_type,
        ),
        in_specs=[
            half_tile,
            half_tile,
            whole((4, 2, 2, PAIR, 128)),
            whole((2, PAIR, 128)),
            whole((3, PAIR, 128)),
            whole((PAIR, 128)),
            shard,
            shard,
            shard,
        ],
        out_specs=(
            pl.BlockSpec((1, INNER, SPAN), lambda e: (e, 0, 0)),
            shard,
            shard,
            shard,
        ),
        scratch_shapes=[
            pltpu.VMEM((A_BLOCKS * SHARD, COLS), F32),
            pltpu.VMEM((INNER, COLS), BF16),
            pltpu.VMEM((SPAN, COLS), BF16),
            pltpu.VMEM((3 * SHARD, COLS), F32),
        ],
        compiler_params=pltpu.CompilerParams(vmem_limit_bytes=32 * 2**20),
    )(*operands)


def body(
    hidden,
    slot_token,
    gate,
    counts,
    cotangent,
    halfwidth_replica,
    precise_matrices,
    running_mean,
    running_variance,
    base,
):
    base_other, fresh_main, fresh_extra, fresh_second, grad_total = exchange(
        hidden,
        slot_token,
        gate,
        counts.reshape(1, EXPERTS),
        cotangent,
        halfwidth_replica,
        precise_matrices,
        running_mean,
        running_variance,
        base,
    )
    return merge(
        base,
        base_other,
        fresh_main,
        fresh_extra,
        fresh_second,
        grad_total,
        precise_matrices,
        running_mean,
        running_variance,
    )


def solution(mesh):
    in_specs = (
        P("expert", ("dp", "rollout"), None),
        P("expert", ("dp", "rollout")),
        P("expert", ("dp", "rollout")),
        P("expert", ("dp", "rollout")),
        P(("dp", "rollout"), None),
        P(None, "expert"),
        P(("dp", "rollout"), "expert"),
        P(("dp", "rollout"), "expert"),
        P(("dp", "rollout"), "expert"),
        P("expert", "rollout", "dp"),
    )
    out_specs = (
        P("expert", None, "dp"),
        P(("dp", "rollout"), "expert"),
        P(("dp", "rollout"), "expert"),
        P(("dp", "rollout"), "expert"),
    )
    return jax.shard_map(body, mesh=mesh, in_specs=in_specs, out_specs=out_specs, check_vma=False)
```

```python
import functools

import jax
import jax.numpy as jnp
from jax import lax
from jax.experimental import pallas as pl
from jax.experimental.pallas import tpu as pltpu
from jax.sharding import PartitionSpec as P

STEP = 100

delta_multiplier = 2.0
beta_first = 0.9
beta_second = 0.95
learn_rate = 0.04
decay_rate = 0.01
adam_eps = 1e-08

MESH = pl.DeviceIdType.MESH
BF16 = jnp.bfloat16
F32 = jnp.float32

EXPERTS = 4
CAP = 320
SLOTS = EXPERTS * CAP
INNER = 1536
WIDE = 4096
TOK = 512
COLS = 256
ROWS = INNER + WIDE
SHARD = 88
PAIR = 2 * SHARD
TILE = 512
SPAN = 128
A_BLOCKS = 18
PIECES = 4
BASE_TURNS = (11, 0, 5)


def adamw_update(derivative_total, precise_matrices, running_mean, running_variance):
    new_first = beta_first * running_mean + (1.0 - beta_first) * derivative_total
    new_second = (
        beta_second * running_variance + (1.0 - beta_second) * derivative_total * derivative_total
    )
    first_hat = new_first / (1.0 - beta_first**STEP)
    second_hat = new_second / (1.0 - beta_second**STEP)
    revised_precise = precise_matrices - learn_rate * (
        first_hat / (jnp.sqrt(second_hat) + adam_eps) + decay_rate * precise_matrices
    )
    return (revised_precise, new_first, new_second)


def fold(block):
    return jnp.concatenate([block[:, :128], block[:, 128:]], axis=0)


def unfold(block):
    return jnp.concatenate([block[:SHARD], block[SHARD:]], axis=1)


def dot(lhs, rhs):
    return jnp.dot(lhs, rhs, preferred_element_type=F32)


def dot_t(lhs, rhs):
    return lax.dot_general(lhs, rhs, (((0,), (0,)), ((), ())), preferred_element_type=F32)


def split(value):
    high = value.astype(BF16)
    return high, (value - high.astype(F32)).astype(BF16)


def exchange_kernel(
    hidden,
    slot_token,
    gate,
    counts,
    cotangent,
    factors,
    precise,
    mean,
    variance,
    base,
    base_other,
    fresh_main,
    fresh_extra,
    fresh_second,
    grad_out,
    hid,
    cot,
    fac,
    tok_v,
    gate_v,
    counts_v,
    opt_v,
    select,
    slots_v,
    grad,
    from_core,
    y_send,
    y_recv,
    z_keep,
    z_send,
    z_recv,
    fresh,
    load_sem,
    local_sem,
    base_send_sem,
    base_recv_sem,
    core_send_sem,
    core_recv_sem,
    y_send_sem,
    y_recv_sem,
    z_send_sem,
    z_recv_sem,
    az_send_sem,
    az_recv_sem,
    ay_send_sem,
    ay_recv_sem,
    ac_send_sem,
    ac_recv_sem,
    b_send_sem,
    b_recv_sem,
):
    dp = lax.axis_index("dp")
    half = lax.axis_index("rollout")
    core = lax.rem(dp, 2)
    row = lax.rem(lax.div(dp, 2), 4)
    low = lax.div(dp, 8)
    z = half * 4 + low
    mine = dp * 2 + half

    def device(c, y, zz):
        return {"dp": lax.rem(zz, 4) * 8 + y * 2 + c, "rollout": lax.div(zz, 4)}

    def at_y(step):
        return lax.rem(row + step, 4)

    def at_z(step):
        return lax.rem(z + step, 8)

    def remote(src, dst, send, recv, target):
        return pltpu.make_async_remote_copy(
            src_ref=src,
            dst_ref=dst,
            send_sem=send,
            recv_sem=recv,
            device_id=target,
            device_id_type=MESH,
        )

    loads = []

    def load(src, dst):
        copy = pltpu.make_async_copy(src, dst, load_sem.at[len(loads)])
        copy.start()
        loads.append(copy)
        return copy

    load_c = load(cotangent, cot)
    load_b = load(factors.at[pl.ds(INNER, WIDE)], fac.at[pl.ds(INNER, WIDE)])
    load_small = [load(slot_token, tok_v), load(gate, gate_v), load(counts, counts_v)]
    load_h = [
        load(hidden.at[e], hid.at[pl.ds(e * CAP, CAP)]) for e in range(EXPERTS)
    ]
    load_a = load(factors.at[pl.ds(0, INNER)], fac.at[pl.ds(0, INNER)])
    load_o = [
        load(precise, opt_v.at[0]),
        load(mean, opt_v.at[1]),
        load(variance, opt_v.at[2]),
    ]

    sends = []
    first_row = mine * SHARD - INNER
    first_user = lax.div(jnp.maximum(first_row, 0), SPAN)
    last_user = lax.div(jnp.maximum(first_row + SHARD - 1, 0), SPAN)
    has_second = first_row + SHARD > 0
    for q, user in enumerate((first_user, last_user)):
        wanted = has_second if q == 0 else jnp.logical_and(has_second, last_user != first_user)
        slot = mine - lax.div(INNER + SPAN * user, SHARD)
        for t in range(2):
            own = jnp.logical_and(user == dp, half == t)
            sends.append((user, t, slot, wanted, own))
    first_block = lax.div(INNER + SPAN * dp, SHARD)
    takes = []
    for j in range(3):
        block = first_block + j
        wanted = block * SHARD < INNER + SPAN * dp + SPAN
        takes.append((block, wanted, block == mine))

    barrier = pltpu.get_barrier_semaphore()

    def greet(target):
        pl.semaphore_signal(barrier, inc=1, device_id=target, device_id_type=MESH)

    greet(device(1 - core, row, z))
    for step in range(1, 4):
        greet(device(core, at_y(step), z))
    for step in range(1, 8):
        greet(device(core, row, at_z(step)))
    for user, t, slot, wanted, own in sends:

        @pl.when(jnp.logical_and(wanted, jnp.logical_not(own)))
        def _():
            greet({"dp": user, "rollout": t})

    for block, wanted, own in takes:

        @pl.when(jnp.logical_and(wanted, jnp.logical_not(own)))
        def _():
            greet({"dp": lax.div(block, 2), "rollout": lax.rem(block, 2)})

    greeted = 11
    for wanted, own in [s[3:] for s in sends] + [t[1:] for t in takes]:
        greeted = greeted + jnp.where(jnp.logical_and(wanted, jnp.logical_not(own)), 1, 0)
    pl.semaphore_wait(barrier, greeted)

    def base_copy(piece):
        rows = INNER // 2 // PIECES
        place = (piece // PIECES, pl.ds(piece % PIECES * rows, rows))
        return remote(
            base.at[place],
            base_other.at[place],
            base_send_sem.at[piece],
            base_recv_sem.at[piece],
            device(core, row, at_z(4)),
        )

    def send_base(turn):
        first = sum(BASE_TURNS[:turn])
        for piece in range(first, first + BASE_TURNS[turn]):
            base_copy(piece).start()

    send_base(0)

    for copy in load_small:
        copy.wait()
    places = lax.broadcasted_iota(jnp.int32, (1, CAP), 1)
    tokens = lax.broadcasted_iota(jnp.int32, (TOK, CAP), 0)
    for e in range(EXPERTS):
        live_gate = jnp.where(places < counts_v[0, e], gate_v[e : e + 1], 0.0)
        gate_high = live_gate.astype(BF16).astype(F32)
        gate_low = live_gate - gate_high
        hit = tokens == tok_v[e : e + 1]
        for part, value in enumerate((gate_high, gate_low)):
            select[e, part] = jnp.where(hit, value, 0.0).astype(BF16)
    lanes = lax.broadcasted_iota(jnp.int32, (CAP, COLS), 1)
    load_c.wait()
    load_b.wait()
    back_high, back_low = split(dot(cot[...], fac[INNER:]))
    for e in range(EXPERTS):
        inside = jnp.logical_and(lanes >= e * 64, lanes < (e + 1) * 64)
        back = (
            dot_t(select[e, 0], back_high)
            + dot_t(select[e, 1], back_high)
            + dot_t(select[e, 0], back_low)
        )
        slots_v[e * CAP : (e + 1) * CAP] = jnp.where(inside, back, 0.0).astype(BF16)

    def core_copy(chunk):
        return remote(
            grad.at[pl.ds(pl.multiple_of(352 * chunk + PAIR * (1 - core), 8), PAIR)],
            from_core.at[chunk],
            core_send_sem.at[chunk],
            core_recv_sem.at[chunk],
            device(1 - core, row, z),
        )

    def own_rows(chunk):
        return grad[pl.ds(pl.multiple_of(352 * chunk + PAIR * core, 8), PAIR)]

    side = 1 - 2 * core

    def y_copy(g, slot):
        way = -side if slot == 1 else side
        return remote(
            y_send.at[g, slot],
            y_recv.at[g, slot],
            y_send_sem.at[g, slot],
            y_recv_sem.at[g, slot],
            device(core, at_y(way + 4), z),
        )

    def to_core(g):
        for chunk in range(4 * g, 4 * g + 4):
            core_copy(chunk).start()

    def core_sum(g, step):
        chunk = 4 * g + at_y(step)
        return own_rows(chunk) + from_core[chunk]

    def to_y(g):
        for chunk in range(4 * g, 4 * g + 4):
            core_copy(chunk).wait_recv()
        for slot, step in ((0, 2), (1, 4 - side)):
            y_send[g, slot] = core_sum(g, step).astype(BF16)
            y_copy(g, slot).start()

    def on_along_y(g):
        y_copy(g, 0).wait_recv()
        y_send[g, 2] = (core_sum(g, 4 + side) + y_recv[g, 0].astype(F32)).astype(BF16)
        y_copy(g, 2).start()

    for copy in load_h:
        copy.wait()
    for tile in range(3):
        grad[tile * TILE : (tile + 1) * TILE] = dot_t(
            hid[:, tile * TILE : (tile + 1) * TILE], slots_v[...]
        )
    to_core(0)

    load_a.wait()
    by_token = jnp.zeros((TOK, COLS), F32)
    for e in range(EXPERTS):
        down = dot(hid[e * CAP : (e + 1) * CAP], fac[:INNER])
        inside = jnp.logical_and(lanes >= e * 64, lanes < (e + 1) * 64)
        down = jnp.where(inside, down, 0.0).astype(BF16)
        by_token = by_token + dot(select[e, 0], down) + dot(select[e, 1], down)
    token_high, token_low = split(by_token)
    to_y(0)

    def second_tile(tile):
        lhs = cot[:, tile * TILE : (tile + 1) * TILE]
        grad[INNER + tile * TILE : INNER + (tile + 1) * TILE] = dot_t(lhs, token_high) + dot_t(
            lhs, token_low
        )

    for tile in range(0, 3):
        second_tile(tile)
    to_core(1)
    for tile in range(3, 6):
        second_tile(tile)
    to_core(2)
    to_y(1)
    on_along_y(0)
    for tile in range(6, 8):
        second_tile(tile)
    to_core(3)
    to_y(2)
    on_along_y(1)
    to_y(3)
    on_along_y(2)
    on_along_y(3)

    def z_copy(step_index, block, target):
        return remote(
            z_send.at[block],
            z_recv.at[step_index],
            z_send_sem.at[step_index],
            z_recv_sem.at[step_index],
            device(core, row, target),
        )

    def to_z(g):
        total = core_sum(g, 0)
        for slot in (1, 2):
            y_copy(g, slot).wait_recv()
            total = total + y_recv[g, slot].astype(F32)
        for h in range(2):
            target = 4 * h + g
            block = fold(total[h * SHARD : (h + 1) * SHARD])
            z_keep[target] = block
            z_send[target] = block.astype(BF16)

    grad_copy = pltpu.make_async_copy(z_keep.at[8], grad_out, local_sem.at[5])

    def b_copy(q):
        user, t, slot = sends[q][:3]
        return remote(
            fresh,
            fresh_second.at[slot],
            b_send_sem.at[q],
            b_recv_sem.at[slot],
            {"dp": user, "rollout": t},
        )

    def update():
        derivative = z_keep[z]
        for step in range(1, 8):
            z_copy(step - 1, at_z(step), at_z(step)).wait_recv()
            derivative = derivative + z_recv[step - 1].astype(F32)
        derivative = delta_multiplier * derivative
        z_keep[8] = derivative
        revised, unused_first, unused_second = adamw_update(
            unfold(derivative), opt_v[0], opt_v[1], opt_v[2]
        )
        fresh[...] = fold(revised).astype(BF16)
        grad_copy.start()

    def send_second(q):
        user, t, slot, wanted, own = sends[q]

        @pl.when(jnp.logical_and(wanted, jnp.logical_not(own)))
        def _():
            b_copy(q).start()

        @pl.when(jnp.logical_and(wanted, own))
        def _():
            local = pltpu.make_async_copy(fresh, fresh_second.at[slot], local_sem.at[0])
            local.start()
            local.wait()

    is_extra = jnp.logical_and(row == 0, core == 0)
    sends_main = low == 0
    sends_extra = jnp.logical_and(low == 1, is_extra)

    def main_place(y, c, h):
        return fresh_main.at[y, c, h]

    def az_copy(step, dst, sem):
        return remote(
            fresh, dst, az_send_sem.at[step - 1], az_recv_sem.at[sem], device(core, row, at_z(step))
        )

    for copy in load_o:
        copy.wait()
    for g in range(4):
        to_z(g)
    for step in (4, 3, 5, 2, 6, 1, 7):
        z_copy(step - 1, at_z(step), at_z(step)).start()
    send_base(1)
    update()

    @pl.when(low == 0)
    def _():
        for step in range(1, 8):
            az_copy(step, main_place(row, core, half), half).start()
        local = pltpu.make_async_copy(fresh, main_place(row, core, half), local_sem.at[1])
        local.start()
        local.wait()

    @pl.when(sends_extra)
    def _():
        for step in range(1, 8):
            az_copy(step, fresh_extra.at[half], 2 + half).start()
        local = pltpu.make_async_copy(fresh, fresh_extra.at[half], local_sem.at[2])
        local.start()
        local.wait()

    for q in range(len(sends)):
        send_second(q)

    send_base(2)

    for h in range(2):

        @pl.when(z != 4 * h)
        def _():
            az_copy(1, main_place(row, core, h), h).wait_recv()

    def ay_copy(y, step):
        return remote(
            fresh_main.at[y, core],
            fresh_main.at[y, core],
            ay_send_sem.at[step - 1],
            ay_recv_sem.at[step - 1],
            device(core, at_y(step), z),
        )

    def ac_copy(y, c):
        return remote(
            fresh_main.at[y, c],
            fresh_main.at[y, c],
            ac_send_sem.at[y],
            ac_recv_sem.at[y],
            device(1 - core, row, z),
        )

    for step in (2, 1, 3):
        ay_copy(row, step).start()
    ac_copy(row, core).start()

    def ey_copy(step):
        return remote(
            fresh_extra,
            fresh_extra,
            ay_send_sem.at[2 + step],
            ay_recv_sem.at[3],
            device(core, at_y(step), z),
        )

    def ec_copy():
        return remote(
            fresh_extra, fresh_extra, ac_send_sem.at[4], ac_recv_sem.at[4], device(1 - core, row, z)
        )

    @pl.when(is_extra)
    def _():
        for h in range(2):

            @pl.when(z != 4 * h + 1)
            def _():
                az_copy(1, fresh_extra.at[h], 2 + h).wait_recv()

        for step in range(1, 4):
            ey_copy(step).start()
        ec_copy().start()

    for step in (1, 3, 2):
        source = lax.rem(row - step + 4, 4)
        ay_copy(source, step).wait_recv()
        ac_copy(source, core).start()

    @pl.when(jnp.logical_and(row != 0, core == 0))
    def _():
        ey_copy(1).wait_recv()
        ec_copy().start()

    for step in range(4):
        ac_copy(at_y(step), 1 - core).wait_recv()

    @pl.when(core == 1)
    def _():
        ec_copy().wait_recv()

    for j, (block, wanted, own) in enumerate(takes):

        @pl.when(jnp.logical_and(wanted, jnp.logical_not(own)))
        def _():
            remote(
                fresh,
                fresh_second.at[j],
                b_send_sem.at[0],
                b_recv_sem.at[j],
                {"dp": lax.div(block, 2), "rollout": lax.rem(block, 2)},
            ).wait_recv()

    for chunk in range(16):
        core_copy(chunk).wait_send()
    for g in range(4):
        for slot in range(3):
            y_copy(g, slot).wait_send()
    for step in range(1, 8):
        z_copy(step - 1, at_z(step), at_z(step)).wait_send()
    for q, (user, t, slot, wanted, own) in enumerate(sends):

        @pl.when(jnp.logical_and(wanted, jnp.logical_not(own)))
        def _():
            b_copy(q).wait_send()

    @pl.when(jnp.logical_or(sends_main, sends_extra))
    def _():
        for step in range(1, 8):
            az_copy(step, fresh_extra.at[half], 0).wait_send()

    for step in range(1, 4):
        ay_copy(row, step).wait_send()
    for y in range(4):
        ac_copy(y, core).wait_send()

    @pl.when(is_extra)
    def _():
        for step in range(1, 4):
            ey_copy(step).wait_send()

    @pl.when(core == 0)
    def _():
        ec_copy().wait_send()

    grad_copy.wait()
    for piece in range(EXPERTS * PIECES):
        base_copy(piece).wait()


def exchange(*operands):
    any_space = pl.BlockSpec(memory_space=pl.ANY)
    dma = pltpu.SemaphoreType.DMA
    return pl.pallas_call(
        exchange_kernel,
        out_shape=(
            pltpu.VMEM((EXPERTS, INNER // 2, SPAN), BF16),
            pltpu.VMEM((4, 2, 2, PAIR, 128), BF16),
            pltpu.VMEM((2, PAIR, 128), BF16),
            pltpu.VMEM((3, PAIR, 128), BF16),
            pltpu.VMEM((PAIR, 128), F32),
        ),
        in_specs=[any_space] * len(operands),
        out_specs=(any_space,) * 5,
        scratch_shapes=[
            pltpu.VMEM((SLOTS, INNER), BF16),
            pltpu.VMEM((TOK, WIDE), BF16),
            pltpu.VMEM((ROWS, COLS), BF16),
            pltpu.VMEM((EXPERTS, CAP), jnp.int32),
            pltpu.VMEM((EXPERTS, CAP), F32),
            pltpu.SMEM((1, EXPERTS), jnp.int32),
            pltpu.VMEM((3, SHARD, COLS), F32),
            pltpu.VMEM((EXPERTS, 2, TOK, CAP), BF16),
            pltpu.VMEM((SLOTS, COLS), BF16),
            pltpu.VMEM((ROWS, COLS), F32),
            pltpu.VMEM((16, PAIR, COLS), F32),
            pltpu.VMEM((4, 3, PAIR, COLS), BF16),
            pltpu.VMEM((4, 3, PAIR, COLS), BF16),
            pltpu.VMEM((9, PAIR, 128), F32),
            pltpu.VMEM((8, PAIR, 128), BF16),
            pltpu.VMEM((7, PAIR, 128), BF16),
            pltpu.VMEM((PAIR, 128), BF16),
            dma((13,)),
            dma((6,)),
            dma((EXPERTS * PIECES,)),
            dma((EXPERTS * PIECES,)),
            dma((16,)),
            dma((16,)),
            dma((4, 3)),
            dma((4, 3)),
            dma((7,)),
            dma((7,)),
            dma((7,)),
            dma((4,)),
            dma((6,)),
            dma((4,)),
            dma((5,)),
            dma((5,)),
            dma((4,)),
            dma((3,)),
        ],
        compiler_params=pltpu.CompilerParams(
            collective_id=0, has_side_effects=True, vmem_limit_bytes=60 * 2**20
        ),
    )(*operands)


def merge_kernel(
    base_own,
    base_other,
    fresh_main,
    fresh_extra,
    fresh_second,
    grad_total,
    precise,
    mean,
    variance,
    merged,
    revised_out,
    first_out,
    second_out,
    wide,
    first,
    second,
    near,
):
    e = pl.program_id(0)
    dp = lax.axis_index("dp")
    half = lax.axis_index("rollout")

    @pl.when(e == 0)
    def _():
        for block in range(A_BLOCKS):
            if block < 16:
                folded = fresh_main[block // 4, (block // 2) % 2, block % 2]
            else:
                folded = fresh_extra[block - 16]
            wide[block * SHARD : (block + 1) * SHARD] = unfold(folded.astype(F32))
        first[...] = wide[:INNER].astype(BF16)
        for j in range(3):
            near[j * SHARD : (j + 1) * SHARD] = unfold(fresh_second[j].astype(F32))
        skip = INNER + SPAN * dp - lax.div(INNER + SPAN * dp, SHARD) * SHARD
        second[...] = near[pl.ds(pl.multiple_of(skip, 8), SPAN)].astype(BF16)
        revised, new_first, new_second = adamw_update(
            unfold(grad_total[...]), precise[...], mean[...], variance[...]
        )
        revised_out[...] = revised
        first_out[...] = new_first
        second_out[...] = new_second

    lanes = lax.broadcasted_iota(jnp.int32, (SPAN, COLS), 1)
    inside = jnp.logical_and(lanes >= e * 64, lanes < (e + 1) * 64)
    columns = jnp.where(inside, second[...].astype(F32), 0.0).astype(BF16)
    for part, tile in ((half, base_own), (1 - half, base_other)):
        rows = pl.ds(pl.multiple_of(part * (INNER // 2), 256), INNER // 2)
        product = lax.dot_general(
            first[rows], columns, (((1,), (1,)), ((), ())), preferred_element_type=F32
        )
        merged[0, rows] = (tile[0].astype(F32) + delta_multiplier * product).astype(BF16)


def merge(*operands):
    half_tile = pl.BlockSpec((1, INNER // 2, SPAN), lambda e: (e, 0, 0))

    def whole(shape):
        return pl.BlockSpec(shape, lambda e: (0,) * len(shape))

    shard = whole((SHARD, COLS))
    shard_type = jax.ShapeDtypeStruct((SHARD, COLS), F32)
    return pl.pallas_call(
        merge_kernel,
        grid=(EXPERTS,),
        out_shape=(
            jax.ShapeDtypeStruct((EXPERTS, INNER, SPAN), BF16),
            shard_type,
            shard_type,
            shard_type,
        ),
        in_specs=[
            half_tile,
            half_tile,
            whole((4, 2, 2, PAIR, 128)),
            whole((2, PAIR, 128)),
            whole((3, PAIR, 128)),
            whole((PAIR, 128)),
            shard,
            shard,
            shard,
        ],
        out_specs=(
            pl.BlockSpec((1, INNER, SPAN), lambda e: (e, 0, 0)),
            shard,
            shard,
            shard,
        ),
        scratch_shapes=[
            pltpu.VMEM((A_BLOCKS * SHARD, COLS), F32),
            pltpu.VMEM((INNER, COLS), BF16),
            pltpu.VMEM((SPAN, COLS), BF16),
            pltpu.VMEM((3 * SHARD, COLS), F32),
        ],
        compiler_params=pltpu.CompilerParams(vmem_limit_bytes=32 * 2**20),
    )(*operands)


def body(
    hidden,
    slot_token,
    gate,
    counts,
    cotangent,
    halfwidth_replica,
    precise_matrices,
    running_mean,
    running_variance,
    base,
):
    base_other, fresh_main, fresh_extra, fresh_second, grad_total = exchange(
        hidden,
        slot_token,
        gate,
        counts.reshape(1, EXPERTS),
        cotangent,
        halfwidth_replica,
        precise_matrices,
        running_mean,
        running_variance,
        base,
    )
    return merge(
        base,
        base_other,
        fresh_main,
        fresh_extra,
        fresh_second,
        grad_total,
        precise_matrices,
        running_mean,
        running_variance,
    )


def solution(mesh):
    in_specs = (
        P("expert", ("dp", "rollout"), None),
        P("expert", ("dp", "rollout")),
        P("expert", ("dp", "rollout")),
        P("expert", ("dp", "rollout")),
        P(("dp", "rollout"), None),
        P(None, "expert"),
        P(("dp", "rollout"), "expert"),
        P(("dp", "rollout"), "expert"),
        P(("dp", "rollout"), "expert"),
        P("expert", "rollout", "dp"),
    )
    out_specs = (
        P("expert", None, "dp"),
        P(("dp", "rollout"), "expert"),
        P(("dp", "rollout"), "expert"),
        P(("dp", "rollout"), "expert"),
    )
    return jax.shard_map(body, mesh=mesh, in_specs=in_specs, out_specs=out_specs, check_vma=False)
```
